512 devices in a mesh: hid: 64 (over z, y), wid: 8 (over x, core).
Axes of the slice: x: 4, y: 8, z: 8, core: 2. Of those that a mesh axis runs over, the one named last changes fastest.
Arguments:
- tokens: bfloat16 [256, 12288], P('hid', 'wid'), may hold values from -6 to 6
- out_grad: bfloat16 [256, 12288], P('hid', 'wid'), may hold values from -6 to 6
- up_tiles: bfloat16 [64, 8, 18, 128, 128], P('hid', 'wid'), may hold values from -0.109375 to 0.109375
- down_tiles: bfloat16 [64, 8, 18, 128, 128], P('hid', 'wid'), may hold values from -0.0546875 to 0.0546875
- up_slots: int32 [64, 8, 18], P('hid', 'wid'), may hold values from 0 to 71, as said below
- down_slots: int32 [64, 8, 18], P('hid', 'wid'), may hold values from 0 to 71, as said below
Outputs:
- mixed: bfloat16 [256, 12288], P('hid', 'wid')
- grad_tokens: bfloat16 [256, 12288], P('hid', 'wid')
- grad_up: float32 [64, 8, 18, 128, 128], P('hid', 'wid')
- grad_down: float32 [64, 8, 18, 128, 128], P('hid', 'wid')
The draws below stay inside these ranges and needn't reach their ends.
Inputs may be any that keep to these rules, and one draw needn't show every extreme that they name: `up_slots`: on each device the 18 positions are distinct and ascending, a quarter of the 72 positions. `down_slots`: on each device the 18 positions are distinct and ascending, a quarter of the 72 positions.
All inputs are finite; a program needn't handle non-finite values.
Results may differ from the reference program's by a relative error of at most 0.0049.
Values may be sent and summed in bfloat16 or wider, within the bound.
A program may use at most 64 MiB of HBM per device.

```python
import jax
import jax.numpy as jnp
from jax import lax

D = 12288
FF = 49152
TILE = 128
TOKENS = 256
ROW_TILES = 12
HID_BLOCKS = 6
SLOTS = 72
TILES_DEV = 18
N_HID = 64
N_WID = 8


def pick_slots(key):
    ranking = jax.random.randint(key, (N_HID, N_WID, SLOTS), 0, 1 << 20) * SLOTS + jnp.arange(SLOTS, dtype=jnp.int32)
    placing = jnp.argsort(ranking, axis=-1)
    return jnp.sort(placing[..., :TILES_DEV], axis=-1).astype(jnp.int32)


def draw_up_slots(key, part):
    key = jax.random.fold_in(key, 11)
    return pick_slots(key)


def draw_down_slots(key, part):
    key = jax.random.fold_in(key, 23)
    return pick_slots(key)


def shard_levels(stream_key, dims, cuts, low, high):
    gain = 1.0
    for axis_at, blocks in cuts:
        heights = jax.random.uniform(jax.random.fold_in(jax.random.fold_in(stream_key, 6), axis_at), (blocks,), jnp.float32, low / len(cuts), high / len(cuts))
        gain = gain * jnp.repeat(jnp.exp(heights), dims[axis_at] // blocks).reshape((-1,) + (1,) * (len(dims) - 1 - axis_at))
    return gain


def gaussian(rng, dims, scale, bound, split=(), kind=jnp.bfloat16):
    loudness = shard_levels(rng, dims, split, -0.22, 0.18) if split else 1.0
    values = jax.random.normal(rng, dims, jnp.float32) * scale * loudness
    return jnp.minimum(jnp.maximum(values, -bound), bound).astype(kind)


def setup_inputs(seed: int = 0) -> dict:
    streams_of = jax.random.split(jax.random.key(seed), 7)
    tokens = gaussian(streams_of[0], (TOKENS, D), 1.0, 6.0, ((0, 64), (1, 8)))
    out_grad = gaussian(streams_of[1], (TOKENS, D), 1.0, 6.0, ((0, 64), (1, 8)))
    up_tiles = gaussian(streams_of[2], (N_HID, N_WID, TILES_DEV, TILE, TILE), (D // 4) ** -0.5, 0.109375, ((0, 64), (1, 8)))
    down_tiles = gaussian(streams_of[3], (N_HID, N_WID, TILES_DEV, TILE, TILE), (FF // 4) ** -0.5, 0.0546875, ((0, 64), (1, 8)))
    up_slots = draw_up_slots(jax.random.fold_in(streams_of[6], 71), 0)
    down_slots = draw_down_slots(jax.random.fold_in(streams_of[6], 71), 0)
    return dict(tokens=tokens, out_grad=out_grad, up_tiles=up_tiles, down_tiles=down_tiles, up_slots=up_slots, down_slots=down_slots)


highest = lax.Precision.HIGHEST
root_coef = 0.7978845608028654
cubic_coef = 0.044715


def gelu_value(value):
    inner = jnp.tanh(root_coef * (value + cubic_coef * value * value * value))
    return 0.5 * value * (1.0 + inner)


def gelu_slope(value):
    inner = jnp.tanh(root_coef * (value + cubic_coef * value * value * value))
    return 0.5 * (1.0 + inner) + 0.5 * value * (1.0 - inner * inner) * root_coef * (1.0 + 3.0 * cubic_coef * value * value)


def one_hot(values, count):
    return (values[:, None] == jnp.arange(count, dtype=jnp.int32)[None, :]).astype(jnp.float32)


def reference(tokens, out_grad, up_tiles, down_tiles, up_slots, down_slots):
    col_count = D // TILE
    token_blocks = tokens.reshape(TOKENS, col_count, TILE)
    grad_blocks = out_grad.reshape(TOKENS, col_count, TILE)
    shard_base = (jnp.arange(N_WID, dtype=jnp.int32) * ROW_TILES)[:, None]

    def column_step(carry, pieces):
        mixed_sum, input_sum = carry
        up_tile, down_tile, up_slot, down_slot = pieces
        up_tile = up_tile.reshape(N_WID * TILES_DEV, TILE, TILE).astype(jnp.float32)
        down_tile = down_tile.reshape(N_WID * TILES_DEV, TILE, TILE).astype(jnp.float32)
        up_rows = (shard_base + up_slot // HID_BLOCKS).reshape(-1).astype(jnp.int32)
        up_block = (up_slot % HID_BLOCKS).reshape(-1).astype(jnp.int32)
        down_block = (down_slot // ROW_TILES).reshape(-1).astype(jnp.int32)
        down_cols = (shard_base + down_slot % ROW_TILES).reshape(-1).astype(jnp.int32)
        x_tiles = jnp.take(token_blocks, up_rows, axis=1).astype(jnp.float32)
        grad_tiles = jnp.take(grad_blocks, down_cols, axis=1).astype(jnp.float32)
        up_prod = jnp.einsum("tnk,nkj->tnj", x_tiles, up_tile, precision=highest)
        pre_sum = jnp.einsum("tnj,nb->tbj", up_prod, one_hot(up_block, HID_BLOCKS), precision=highest)
        hidden = gelu_value(pre_sum).astype(jnp.bfloat16)
        back_prod = jnp.einsum("tnj,nkj->tnk", grad_tiles, down_tile, precision=highest)
        back_sum = jnp.einsum("tnk,nb->tbk", back_prod, one_hot(down_block, HID_BLOCKS), precision=highest)
        delta_rows = (back_sum * gelu_slope(pre_sum)).astype(jnp.bfloat16)
        hidden_tiles = jnp.take(hidden, down_block, axis=1).astype(jnp.float32)
        delta_tiles = jnp.take(delta_rows, up_block, axis=1).astype(jnp.float32)
        down_prod = jnp.einsum("tnk,nkj->tnj", hidden_tiles, down_tile, precision=highest)
        mixed_sum = mixed_sum + jnp.einsum("tnj,nc->tcj", down_prod, one_hot(down_cols, col_count), precision=highest).reshape(TOKENS, D)
        input_prod = jnp.einsum("tnj,nkj->tnk", delta_tiles, up_tile, precision=highest)
        input_sum = input_sum + jnp.einsum("tnk,nr->trk", input_prod, one_hot(up_rows, col_count), precision=highest).reshape(TOKENS, D)
        grad_up = jnp.einsum("tnk,tnj->nkj", x_tiles, delta_tiles, precision=highest)
        grad_down = jnp.einsum("tnk,tnj->nkj", hidden_tiles, grad_tiles, precision=highest)
        return (mixed_sum, input_sum), (grad_up.reshape(N_WID, TILES_DEV, TILE, TILE), grad_down.reshape(N_WID, TILES_DEV, TILE, TILE))

    zeros = jnp.zeros((TOKENS, D), jnp.float32)
    (mixed_sum, input_sum), (grad_up, grad_down) = lax.scan(column_step, (zeros, zeros), (up_tiles, down_tiles, up_slots, down_slots))
    return mixed_sum.astype(jnp.bfloat16), input_sum.astype(jnp.bfloat16), grad_up, grad_down
```

```python
import functools

import jax
import jax.numpy as jnp
from jax import lax
from jax.experimental import pallas as pl
from jax.experimental.pallas import tpu as pltpu
from jax.sharding import PartitionSpec as P

MESH = pl.DeviceIdType.MESH
BF = jnp.bfloat16
F32 = jnp.float32

ROOT = 0.7978845608028654
CUBIC = 0.044715


def gelu_both(v):
    inner = jnp.tanh(ROOT * (v + CUBIC * v * v * v))
    value = 0.5 * v * (1.0 + inner)
    slope = 0.5 * (1.0 + inner) + 0.5 * v * (1.0 - inner * inner) * ROOT * (
        1.0 + 3.0 * CUBIC * v * v
    )
    return value, slope


def kernel(
    x_in, g_in, ut_hbm, dt_hbm, us, ds,
    mixed_out, gt_out, gu_hbm, gd_hbm,
    ut, dt, w1, w2, xcar, gcar, flat, xs, gs, xt, gt, htile, dtile, part, rcore, sb, rx, hd,
    mcar, tcar, msend, mrecv, tsend, trecv, ms2, mr2, ts2, tr2, rows4, gu, gd,
    ssem, rsem, lsem,
):
    hid, wid = lax.axis_index("hid"), lax.axis_index("wid")
    z, y = lax.div(hid, 8), lax.rem(hid, 8)
    xx, c = lax.div(wid, 2), lax.rem(wid, 2)

    def at(zz, yy):
        return (lax.rem(zz + 8, 8) * 8 + lax.rem(yy + 8, 8), wid)

    def up8(v):
        return lax.rem(v + 16, 8)

    xpeer = [(hid, lax.rem(xx + o, 4) * 2 + c) for o in (1, 2, 3)]
    partner = (hid, xx * 2 + 1 - c)

    counter = [0]
    sent = []

    def rcopy(src, dst, dev):
        k = counter[0]
        counter[0] += 1
        cp = pltpu.make_async_remote_copy(
            src_ref=src, dst_ref=dst, send_sem=ssem.at[k], recv_sem=rsem.at[k],
            device_id=dev, device_id_type=MESH,
        )
        cp.start()
        sent.append(cp)
        return cp

    load_ut = pltpu.make_async_copy(ut_hbm.at[0, 0], ut, lsem.at[0])
    load_dt = pltpu.make_async_copy(dt_hbm.at[0, 0], dt, lsem.at[1])
    load_ut.start()
    load_dt.start()

    barrier = pltpu.get_barrier_semaphore()
    peers = [at(z, y + o) for o in range(1, 8)] + [at(z + o, y) for o in range(1, 8)]
    peers += xpeer + [partner]
    for dev in peers:
        pl.semaphore_signal(barrier, inc=1, device_id=dev, device_id_type=MESH)

    def to_rows(src, dst):
        val = src[...].astype(F32)
        for r in range(12):
            rows4[4 * r : 4 * r + 4, :] = val[:, r * 128 : (r + 1) * 128]
        dst[...] = rows4[...].astype(BF)

    to_rows(x_in, xcar.at[z, y])
    to_rows(g_in, gcar.at[y, z])
    pl.semaphore_wait(barrier, len(peers))

    first_x = [rcopy(xcar.at[z, y], xcar.at[z, y], at(z, y + o)) for o in range(1, 8)]
    first_g = [rcopy(gcar.at[y, z], gcar.at[y, z], at(z + o, y)) for o in range(1, 8)]

    load_ut.wait()
    load_dt.wait()

    def build(slots, tiles, dense, rows, cols):
        def one(row, carry):
            for col in range(cols):
                spot = row * cols + col
                below, hits = jnp.int32(0), jnp.int32(0)
                for n in range(18):
                    slot = slots[0, 0, n]
                    below = below + (slot < spot).astype(jnp.int32)
                    hits = hits + (slot == spot).astype(jnp.int32)
                tile = tiles[jnp.minimum(below, 17)]
                dense[
                    pl.ds(pl.multiple_of(row * 128, 128), 128), col * 128 : (col + 1) * 128
                ] = jnp.where(hits > 0, tile, jnp.zeros_like(tile))
            return carry

        lax.fori_loop(0, rows, one, jnp.int32(0))

    for cp in first_x + first_g:
        cp.wait_recv()

    right_x, right_g = at(z + 1, y), at(z, y + 1)
    left_x, left_g = at(z - 1, y), at(z, y - 1)
    for s in range(4):
        step = []
        a, b = up8(z - s), up8(y - s)
        step.append(rcopy(xcar.at[a], xcar.at[a], right_x))
        step.append(rcopy(gcar.at[b], gcar.at[b], right_g))
        if s < 3:
            a, b = up8(z + s), up8(y + s)
            step.append(rcopy(xcar.at[a], xcar.at[a], left_x))
            step.append(rcopy(gcar.at[b], gcar.at[b], left_g))
        if s == 0:
            build(us, ut, w1, 12, 6)
        if s == 1:
            build(ds, dt, w2, 6, 12)
        for cp in step:
            cp.wait_recv()

    def spread(src, dst, tiled, zstep, ystep):
        flat[...] = src[...].reshape(3072, 128).astype(F32)

        def one(zz, carry):
            for r in range(12):
                rows = [
                    flat[pl.ds(zz * zstep + 4 * r + i, 8, stride=ystep), :] for i in range(4)
                ]
                val = jnp.concatenate(rows, axis=0).astype(BF)
                span = pl.ds(pl.multiple_of(zz * 32, 32), 32)
                dst[span, r * 128 : (r + 1) * 128] = val
                tiled[r, span, :] = val
            return carry

        lax.fori_loop(0, 8, one, jnp.int32(0))

    spread(xcar, xs, xt, 384, 48)
    pre = jnp.dot(xs[...], w1[...], preferred_element_type=F32)
    part[0, 0] = pre[:, :384]
    part[1, 0] = pre[:, 384:]
    core_x = rcopy(part.at[1 - c, 0], rcore.at[0], partner)
    spread(gcar, gs, gt, 48, 384)
    back = lax.dot_general(
        gs[...], w2[...], (((1,), (1,)), ((), ())), preferred_element_type=F32
    )
    part[0, 1] = back[:, :384]
    part[1, 1] = back[:, 384:]
    core_g = rcopy(part.at[1 - c, 1], rcore.at[1], partner)

    over = []
    for a, cp in ((0, core_x), (1, core_g)):
        cp.wait_recv()
        total = part[c, a] + rcore[a]
        rcore[a] = total
        sb[a] = total.astype(BF).reshape(4, 64, 384)
        for dev, o in zip(xpeer, (1, 2, 3)):
            over.append(rcopy(sb.at[a, lax.rem(xx + o, 4)], rx.at[a, o], dev))
    sums = []
    for a in range(2):
        acc = rcore[a, pl.ds(pl.multiple_of(xx * 64, 64), 64), :]
        for o in (1, 2, 3):
            over[a * 3 + o - 1].wait_recv()
            acc = acc + rx[a, o].astype(F32)
        sums.append(acc)
    value, slope = gelu_both(sums[0])

    def piece(xv, cv):
        return hd.at[
            :, pl.ds(pl.multiple_of(xv * 64, 64), 64), pl.ds(pl.multiple_of(cv * 384, 128), 384)
        ]

    mine = piece(xx, c)
    mine[0] = value.astype(BF)
    mine[1] = (sums[1] * slope).astype(BF)
    spreadx = [rcopy(mine, mine, dev) for dev in xpeer]
    cross = [rcopy(mine, mine, partner)]
    for cp, o in zip(spreadx, (1, 2, 3)):
        cp.wait_recv()
        got = piece(lax.rem(xx + 4 - o, 4), c)
        cross.append(rcopy(got, got, partner))
    for cp in cross:
        cp.wait_recv()

    def gather_rows(val, r, car, zstep, ystep):
        for zz in range(8):
            for i in range(4):
                car[pl.ds(zz * zstep + 4 * r + i, 8, stride=ystep), :] = val[
                    zz * 32 + i * 8 : zz * 32 + i * 8 + 8, :
                ]

    def mixed_cols(q, carry):
        cols = pl.ds(pl.multiple_of(q * 256, 256), 256)
        val = jnp.dot(hd[0], w2[:, cols], preferred_element_type=F32)
        gather_rows(val[:, :128], 2 * q, mcar, 384, 48)
        gather_rows(val[:, 128:], 2 * q + 1, mcar, 384, 48)
        return carry

    def back_cols(q, carry):
        rows = pl.ds(pl.multiple_of(q * 256, 256), 256)
        val = lax.dot_general(
            hd[1], w1[rows, :], (((1,), (1,)), ((), ())), preferred_element_type=F32
        )
        gather_rows(val[:, :128], 2 * q, tcar, 48, 384)
        gather_rows(val[:, 128:], 2 * q + 1, tcar, 48, 384)
        return carry

    def chunk(car, d):
        return car[pl.ds(pl.multiple_of(d * 384, 384), 384), :]

    def ring_send(car, send, recv, pos, right, left, s, prev):
        out = []
        d = up8(pos + 4 - s)
        val = chunk(car, d)
        if s > 0:
            prev[0].wait_recv()
            val = val + recv[0, s - 1].astype(F32)
        send[0, s] = val.astype(BF)
        out.append(rcopy(send.at[0, s], recv.at[0, s], right))
        if s < 3:
            d = up8(pos - 3 + s)
            val = chunk(car, d)
            if s > 0:
                prev[1].wait_recv()
                val = val + recv[1, s - 1].astype(F32)
            send[1, s] = val.astype(BF)
            out.append(rcopy(send.at[1, s], recv.at[1, s], left))
        else:
            out.append(prev[1])
        return out

    lax.fori_loop(0, 6, mixed_cols, jnp.int32(0))
    m_prev = ring_send(mcar, msend, mrecv, z, right_x, left_x, 0, None)
    lax.fori_loop(0, 6, back_cols, jnp.int32(0))
    t_prev = ring_send(tcar, tsend, trecv, y, right_g, left_g, 0, None)

    def one_up(n, carry):
        slot = us[0, 0, n]
        r, b = lax.div(slot, 6), lax.rem(slot, 6)
        lhs, rhs = xt[r], dtile[b]
        gu[n] = lax.dot_general(lhs, rhs, (((0,), (0,)), ((), ())), preferred_element_type=F32)
        return carry

    def one_down(n, carry):
        slot = ds[0, 0, n]
        b, r = lax.div(slot, 12), lax.rem(slot, 12)
        lhs, rhs = htile[b], gt[r]
        gd[n] = lax.dot_general(lhs, rhs, (((0,), (0,)), ((), ())), preferred_element_type=F32)
        return carry

    for b in range(6):
        htile[b] = hd[0, :, b * 128 : (b + 1) * 128]
        dtile[b] = hd[1, :, b * 128 : (b + 1) * 128]

    stores = []
    for s in (1, 2, 3):
        if s == 1:
            lax.fori_loop(0, 18, one_up, jnp.int32(0))
            stores.append(pltpu.make_async_copy(gu, gu_hbm.at[0, 0], lsem.at[2]))
            stores[-1].start()
        if s == 2:
            lax.fori_loop(0, 18, one_down, jnp.int32(0))
            stores.append(pltpu.make_async_copy(gd, gd_hbm.at[0, 0], lsem.at[3]))
            stores[-1].start()
        m_prev = ring_send(mcar, msend, mrecv, z, right_x, left_x, s, m_prev)
        t_prev = ring_send(tcar, tsend, trecv, y, right_g, left_g, s, t_prev)

    def finish_ring(car, recv, pos, prev, send2):
        prev[0].wait_recv()
        prev[1].wait_recv()
        val = chunk(car, pos) + recv[0, 3].astype(F32) + recv[1, 2].astype(F32)
        car[pl.ds(pl.multiple_of(pos * 384, 384), 384), :] = val
        send2[...] = val.astype(BF).reshape(8, 48, 128)

    finish_ring(mcar, mrecv, z, m_prev, ms2)
    last_m = [rcopy(ms2.at[up8(y + o)], mr2.at[o], at(z, y + o)) for o in range(1, 8)]
    finish_ring(tcar, trecv, y, t_prev, ts2)
    last_t = [rcopy(ts2.at[up8(z + o)], tr2.at[o], at(z + o, y)) for o in range(1, 8)]

    def finish(car, base, recv2, last, out):
        acc = car[pl.ds(pl.multiple_of(base, 48), 48), :]
        for o in range(1, 8):
            last[o - 1].wait_recv()
            acc = acc + recv2[o].astype(F32)
        rows4[...] = acc
        cols = [rows4[4 * r : 4 * r + 4, :] for r in range(12)]
        out[...] = jnp.concatenate(cols, axis=1).astype(BF)

    finish(mcar, z * 384 + y * 48, mr2, last_m, mixed_out)
    finish(tcar, y * 384 + z * 48, tr2, last_t, gt_out)

    for cp in sent:
        cp.wait_send()
    for cp in stores:
        cp.wait()


N_COPIES = 14 + 14 + 2 + 6 + 3 + 4 + 14 + 14


def per_device(tokens, out_grad, up_tiles, down_tiles, up_slots, down_slots):
    vmem = pl.BlockSpec(memory_space=pltpu.VMEM)
    smem = pl.BlockSpec(memory_space=pltpu.SMEM)
    hbm = pl.BlockSpec(memory_space=pl.ANY)
    V = pltpu.VMEM
    return pl.pallas_call(
        kernel,
        out_shape=(
            jax.ShapeDtypeStruct((4, 1536), BF),
            jax.ShapeDtypeStruct((4, 1536), BF),
            jax.ShapeDtypeStruct((1, 1, 18, 128, 128), F32),
            jax.ShapeDtypeStruct((1, 1, 18, 128, 128), F32),
        ),
        in_specs=[vmem, vmem, hbm, hbm, smem, smem],
        out_specs=(vmem, vmem, hbm, hbm),
        scratch_shapes=[
            V((18, 128, 128), BF),
            V((18, 128, 128), BF),
            V((1536, 768), BF),
            V((768, 1536), BF),
            V((8, 8, 48, 128), BF),
            V((8, 8, 48, 128), BF),
            V((3072, 128), F32),
            V((256, 1536), BF),
            V((256, 1536), BF),
            V((12, 256, 128), BF),
            V((12, 256, 128), BF),
            V((6, 256, 128), BF),
            V((6, 256, 128), BF),
            V((2, 2, 256, 384), F32),
            V((2, 256, 384), F32),
            V((2, 4, 64, 384), BF),
            V((2, 4, 64, 384), BF),
            V((2, 256, 768), BF),
            V((3072, 128), F32),
            V((3072, 128), F32),
            V((2, 4, 384, 128), BF),
            V((2, 4, 384, 128), BF),
            V((2, 4, 384, 128), BF),
            V((2, 4, 384, 128), BF),
            V((8, 48, 128), BF),
            V((8, 48, 128), BF),
            V((8, 48, 128), BF),
            V((8, 48, 128), BF),
            V((48, 128), F32),
            V((18, 128, 128), F32),
            V((18, 128, 128), F32),
            pltpu.SemaphoreType.DMA((N_COPIES,)),
            pltpu.SemaphoreType.DMA((N_COPIES,)),
            pltpu.SemaphoreType.DMA((4,)),
        ],
        compiler_params=pltpu.CompilerParams(
            collective_id=0, has_side_effects=True, vmem_limit_bytes=48 * 1024 * 1024
        ),
    )(tokens, out_grad, up_tiles, down_tiles, up_slots, down_slots)


def solution(mesh):
    spec2, spec5, spec3 = P("hid", "wid"), P("hid", "wid", None, None, None), P("hid", "wid", None)
    return jax.shard_map(
        per_device,
        mesh=mesh,
        in_specs=(spec2, spec2, spec5, spec5, spec3, spec3),
        out_specs=(spec2, spec2, spec5, spec5),
        check_vma=False,
    )
```

```python
import jax
import jax.numpy as jnp
from jax import lax
from jax.experimental import pallas as pl
from jax.experimental.pallas import tpu as pltpu
from jax.sharding import PartitionSpec as P

MESH = pl.DeviceIdType.MESH
BF = jnp.bfloat16
F32 = jnp.float32

ROOT = 0.7978845608028654
CUBIC = 0.044715

NEAR = (0, 1, 3, 2)
FAR = (2, 3, 1, 0)


def gelu_both(v):
    inner = jnp.tanh(ROOT * (v + CUBIC * v * v * v))
    value = 0.5 * v * (1.0 + inner)
    slope = 0.5 * (1.0 + inner) + 0.5 * v * (1.0 - inner * inner) * ROOT * (
        1.0 + 3.0 * CUBIC * v * v
    )
    return value, slope


def up8(v):
    return lax.rem(v + 16, 8)


def drain(sent, stores):
    for cp in sent:
        cp.wait_send()
    for cp in stores:
        cp.wait()


def kernel(
    x_hbm, g_hbm, ut_hbm, dt_hbm, us_hbm, ds_hbm,
    mixed_out, gt_out, gu_hbm, gd_hbm,
    x_in, g_in, us, ds, ut, dt, w1, w2, xcar, gcar, xflat, gflat, xs, gs, xt, gt,
    part, rcore, sb, rx, hb, db, slopes, backs, htile, dtile,
    mcar, tcar, msend, mrecv, tsend, trecv, ms2, mr2, ts2, tr2, rows4, gu, gd,
    ssem, rsem, lsem,
):
    hid, wid = lax.axis_index("hid"), lax.axis_index("wid")
    z, y = lax.div(hid, 8), lax.rem(hid, 8)
    xx, c = lax.div(wid, 2), lax.rem(wid, 2)

    def at(zz, yy):
        return (up8(zz) * 8 + up8(yy), wid)

    def pair(pos, k):
        q = lax.div(pos, 2)
        return (q, q + 1 - 2 * lax.rem(q, 2), lax.rem(q + 2, 4), 3 - q)[k]

    def mate(pos, k, b):
        low = lax.rem(pos, 2)
        return pair(pos, k) * 2 + (1 - low if b else low)

    others = [(k, b) for k in NEAR for b in (0, 1) if (k, b) != (0, 0)]
    xpeer = [(hid, lax.rem(xx + o, 4) * 2 + c) for o in (1, 2, 3)]
    partner = (hid, xx * 2 + 1 - c)

    counter = [0]
    sent = []
    stores = []

    def rcopy(src, dst, dev):
        k = counter[0]
        counter[0] += 1
        cp = pltpu.make_async_remote_copy(
            src_ref=src, dst_ref=dst, send_sem=ssem.at[k], recv_sem=rsem.at[k],
            device_id=dev, device_id_type=MESH,
        )
        cp.start()
        sent.append(cp)
        return cp

    loads = [
        pltpu.make_async_copy(a, b, lsem.at[n])
        for n, (a, b) in enumerate(
            (
                (x_hbm, x_in), (g_hbm, g_in), (us_hbm, us), (ds_hbm, ds),
                (ut_hbm.at[0, 0], ut), (dt_hbm.at[0, 0], dt),
            )
        )
    ]
    for cp in loads:
        cp.start()

    barrier = pltpu.get_barrier_semaphore()
    peers = [at(z, mate(y, k, b)) for k, b in others] + [at(mate(z, k, b), y) for k, b in others]
    peers += xpeer + [partner]
    for dev in peers:
        pl.semaphore_signal(barrier, inc=1, device_id=dev, device_id_type=MESH)

    def to_rows(src, dst):
        val = src[...].astype(F32)
        for r in range(12):
            rows4[4 * r : 4 * r + 4, :] = val[:, r * 128 : (r + 1) * 128]
        dst[...] = rows4[...].astype(BF)

    loads[0].wait()
    to_rows(x_in, xcar.at[z, y])
    loads[1].wait()
    to_rows(g_in, gcar.at[y, z])
    pl.semaphore_wait(barrier, len(peers))

    first = {}
    for k, b in others:
        first["x", k, b] = rcopy(xcar.at[z, y], xcar.at[z, y], at(z, mate(y, k, b)))
        first["g", k, b] = rcopy(gcar.at[y, z], gcar.at[y, z], at(mate(z, k, b), y))

    for cp in loads[2:]:
        cp.wait()

    def build(slots, tiles, dense, rows, cols):
        def one(row, carry):
            pos = jnp.int32(0)
            for n in range(18):
                pos = pos + (slots[0, 0, n] < row * cols).astype(jnp.int32)
            for col in range(cols):
                idx = jnp.minimum(pos, 17)
                hit = jnp.logical_and(pos < 18, slots[0, 0, idx] == row * cols + col)
                tile = tiles[idx]
                dense[
                    pl.ds(pl.multiple_of(row * 128, 128), 128), col * 128 : (col + 1) * 128
                ] = jnp.where(hit, tile, jnp.zeros_like(tile))
                pos = pos + hit.astype(jnp.int32)
            return carry

        lax.fori_loop(0, rows, one, jnp.int32(0))

    build(us, ut, w1, 12, 6)
    build(ds, dt, w2, 6, 12)

    axes = {
        "x": (xcar, z, y, at(z + 1, y), at(z - 1, y)),
        "g": (gcar, y, z, at(z, y + 1), at(z, y - 1)),
    }
    ring = {}

    def offsets(g):
        return (-g, g + 1)

    def step(s):
        for k in NEAR:
            for name in ("x", "g"):
                car, pos, cross, right, left = axes[name]
                if s == 0:
                    for b in (0, 1):
                        if (k, b) != (0, 0):
                            first[name, k, b].wait_recv()
                else:
                    ring[name, s - 1, k, "r"].wait_recv()
                    if s < 4:
                        ring[name, s - 1, k, "l"].wait_recv()
                span = pl.ds(pair(cross, k) * 2, 2)
                if s < 4:
                    ref = car.at[up8(pos - s), span]
                    ring[name, s, k, "r"] = rcopy(ref, ref, right)
                if s < 3:
                    ref = car.at[up8(pos + s), span]
                    ring[name, s, k, "l"] = rcopy(ref, ref, left)

    def unpack(car, pos, flat, dst, g):
        for off in offsets(g):
            d = up8(pos + off)
            flat[pl.ds(pl.multiple_of(d * 384, 384), 384), :] = (
                car[d].reshape(384, 128).astype(F32)
            )

        def cols(t, carry):
            for u in range(2):
                r = 2 * t + u
                for i in range(4):
                    rows = [
                        flat[pl.ds(up8(pos + off) * 384 + 4 * r + i, 8, stride=48), :]
                        for off in offsets(g)
                    ]
                    dst[g, i * 16 : (i + 1) * 16, pl.ds(pl.multiple_of(r * 128, 128), 128)] = (
                        jnp.concatenate(rows, axis=0).astype(BF)
                    )
            return carry

        lax.fori_loop(0, 6, cols, jnp.int32(0))

    core = {}
    over = {}
    back_home = {}

    def halves(val, g, a):
        part[g, 0, a] = val[:, :384]
        part[g, 1, a] = val[:, 384:]
        core[g, a] = rcopy(part.at[g, 1 - c, a], rcore.at[g, a], partner)

    def compute_x(g):
        unpack(xcar, z, xflat, xs, g)
        halves(jnp.dot(xs[g], w1[...], preferred_element_type=F32), g, 0)

    def compute_g(g):
        unpack(gcar, y, gflat, gs, g)
        halves(
            lax.dot_general(
                gs[g], w2[...], (((1,), (1,)), ((), ())), preferred_element_type=F32
            ),
            g,
            1,
        )

    def sum_cores(g):
        for a in range(2):
            core[g, a].wait_recv()
            total = part[g, c, a] + rcore[g, a]
            rcore[g, a] = total
            for i in range(4):
                sb[g, i, a] = total[i * 16 : (i + 1) * 16].astype(BF)
        for dev, o in zip(xpeer, (1, 2, 3)):
            over[g, o] = rcopy(sb.at[g, lax.rem(xx + o, 4)], rx.at[g, o], dev)

    def mine(buf, g, i):
        return buf.at[
            g,
            pl.ds(pl.multiple_of(i * 16, 16), 16),
            pl.ds(pl.multiple_of(c * 384, 128), 384),
        ]

    def send_home(buf, name, g):
        ref = mine(buf, g, xx)
        back_home[name, g] = [rcopy(ref, ref, dev) for dev in xpeer] + [rcopy(ref, ref, partner)]

    def relay(buf, name, g):
        for n, o in enumerate((1, 2, 3)):
            back_home[name, g][n].wait_recv()
            ref = mine(buf, g, lax.rem(xx + 4 - o, 4))
            back_home[name, g].append(rcopy(ref, ref, partner))

    def all_home(name, g):
        for cp in back_home[name, g][3:]:
            cp.wait_recv()

    def sum_chips(g):
        acc = [rcore[g, a, pl.ds(pl.multiple_of(xx * 16, 16), 16), :] for a in range(2)]
        for o in (1, 2, 3):
            over[g, o].wait_recv()
            acc = [acc[a] + rx[g, o, a].astype(F32) for a in range(2)]
        value, slope = gelu_both(acc[0])
        ref = mine(hb, g, xx)
        ref[...] = value.astype(BF)
        send_home(hb, "h", g)
        for n, off in enumerate(offsets(g)):
            dz, dy = up8(z + off), up8(y + off)
            for t in range(3):
                lanes = slice(t * 128, (t + 1) * 128)
                slopes[t, pl.ds(pl.multiple_of(dz * 8, 8), 8), :] = slope[
                    n * 8 : (n + 1) * 8, lanes
                ]
                backs[t, pl.ds(pl.multiple_of(dy * 8, 8), 8), :] = acc[1][
                    n * 8 : (n + 1) * 8, lanes
                ]

    def delta(g):
        rows = []
        for off in offsets(g):
            dy = up8(y + off)
            rows.append(
                jnp.concatenate(
                    [
                        backs[t, pl.ds(pl.multiple_of(dy * 8, 8), 8), :]
                        * slopes[t, pl.ds(dy, 8, stride=8), :]
                        for t in range(3)
                    ],
                    axis=1,
                )
            )
        ref = mine(db, g, xx)
        ref[...] = jnp.concatenate(rows, axis=0).astype(BF)
        send_home(db, "d", g)

    def retile(flat, pos, dst):
        def one(g, carry):
            for r in range(12):
                for i in range(4):
                    rows = [
                        flat[pl.ds(up8(pos - g + n * (2 * g + 1)) * 48 + 4 * r + i, 8, stride=384), :]
                        for n in range(2)
                    ]
                    dst[r, pl.ds(pl.multiple_of(g * 64 + i * 16, 16), 16), :] = jnp.concatenate(
                        rows, axis=0
                    ).astype(BF)
            return carry

        lax.fori_loop(0, 4, one, jnp.int32(0))

    def pack(val, r, car, pos, groups):
        for n, g in enumerate(groups):
            for i in range(4):
                for m, off in enumerate(offsets(g)):
                    lo = n * 64 + i * 16 + m * 8
                    car[pl.ds(up8(pos + off) * 384 + 4 * r + i, 8, stride=48), :] = val[lo : lo + 8]

    def mixed_part(groups):
        lhs = jnp.concatenate([hb[g] for g in groups], axis=0)

        def cols(q, carry):
            val = jnp.dot(
                lhs, w2[:, pl.ds(pl.multiple_of(q * 256, 256), 256)], preferred_element_type=F32
            )
            pack(val[:, :128], 2 * q, mcar, z, groups)
            pack(val[:, 128:], 2 * q + 1, mcar, z, groups)
            return carry

        lax.fori_loop(0, 6, cols, jnp.int32(0))

    def back_part(groups):
        lhs = jnp.concatenate([db[g] for g in groups], axis=0)

        def cols(q, carry):
            val = lax.dot_general(
                lhs,
                w1[pl.ds(pl.multiple_of(q * 256, 256), 256), :],
                (((1,), (1,)), ((), ())),
                preferred_element_type=F32,
            )
            pack(val[:, :128], 2 * q, tcar, y, groups)
            pack(val[:, 128:], 2 * q + 1, tcar, y, groups)
            return carry

        lax.fori_loop(0, 6, cols, jnp.int32(0))

    outs = {
        "m": (mcar, msend, mrecv, z, y, at(z + 1, y), at(z - 1, y)),
        "t": (tcar, tsend, trecv, y, z, at(z, y + 1), at(z, y - 1)),
    }
    rsum = {}

    def ring_send(name, s):
        car, send, recv, pos, cross, right, left = outs[name]
        for k in FAR:
            at_rows = pair(cross, k) * 96
            span = pl.ds(pl.multiple_of(at_rows, 96), 96)
            for w, dev, d in ((0, right, pos + 4 - s), (1, left, pos - 3 + s)):
                if w == 1 and s == 3:
                    continue
                val = car[pl.ds(pl.multiple_of(up8(d) * 384 + at_rows, 96), 96), :]
                if s > 0:
                    rsum[name, s - 1, k, w].wait_recv()
                    val = val + recv[w, s - 1, span, :].astype(F32)
                send[w, s, span, :] = val.astype(BF)
                rsum[name, s, k, w] = rcopy(
                    send.at[w, s, span, :], recv.at[w, s, span, :], dev
                )

    last = {}

    def ring_end(name, send2, recv2):
        car, send, recv, pos, cross, right, left = outs[name]
        for k in FAR:
            at_rows = pair(cross, k) * 96
            span = pl.ds(pl.multiple_of(at_rows, 96), 96)
            rsum[name, 3, k, 0].wait_recv()
            rsum[name, 2, k, 1].wait_recv()
            here = pl.ds(pl.multiple_of(pos * 384 + at_rows, 96), 96)
            val = car[here, :] + recv[0, 3, span, :].astype(F32) + recv[1, 2, span, :].astype(F32)
            car[here, :] = val
            send2[span, :] = val.astype(BF)
            for b in (0, 1):
                if (k, b) == (0, 0):
                    continue
                to = mate(cross, k, b)
                dev = at(pos, to) if name == "m" else at(to, pos)
                n = 2 * k + b
                last[name, k, b] = rcopy(
                    send2.at[pl.ds(pl.multiple_of(to * 48, 48), 48), :], recv2.at[n], dev
                )

    def one_up(n, carry):
        slot = us[0, 0, n]
        lhs, rhs = xt[lax.div(slot, 6)], dtile[lax.rem(slot, 6)]
        gu[n] = lax.dot_general(lhs, rhs, (((0,), (0,)), ((), ())), preferred_element_type=F32)
        return carry

    def one_down(n, carry):
        slot = ds[0, 0, n]
        lhs, rhs = htile[lax.div(slot, 12)], gt[lax.rem(slot, 12)]
        gd[n] = lax.dot_general(lhs, rhs, (((0,), (0,)), ((), ())), preferred_element_type=F32)
        return carry

    def tile_up(buf, dst):
        for b in range(6):
            dst[b] = buf[:, :, b * 128 : (b + 1) * 128].reshape(256, 128)

    def store(src, dst, n):
        stores.append(pltpu.make_async_copy(src, dst.at[0, 0], lsem.at[n]))
        stores[-1].start()

    step(0)
    step(1)
    compute_x(0)
    compute_g(0)
    step(2)
    sum_cores(0)
    compute_x(1)
    compute_g(1)
    step(3)
    sum_chips(0)
    sum_cores(1)
    compute_x(2)
    compute_g(2)
    step(4)
    compute_x(3)
    compute_g(3)
    sum_cores(2)
    sum_chips(1)
    sum_cores(3)
    relay(hb, "h", 0)
    retile(xflat, y, xt)
    sum_chips(2)
    relay(hb, "h", 1)
    sum_chips(3)
    delta(3)
    for g in (2, 1, 0):
        delta(g)
    relay(hb, "h", 2)
    for g in (0, 1, 2):
        all_home("h", g)
    mixed_part((0, 1, 2))
    relay(hb, "h", 3)
    relay(db, "d", 3)
    all_home("h", 3)
    mixed_part((3,))
    ring_send("m", 0)
    all_home("d", 3)
    back_part((3,))
    ring_send("t", 0)
    for g in (2, 1, 0):
        relay(db, "d", g)
    for g in (2, 1, 0):
        all_home("d", g)
    back_part((2, 1, 0))
    ring_send("m", 1)
    ring_send("t", 1)
    tile_up(db, dtile)
    lax.fori_loop(0, 18, one_up, jnp.int32(0))
    store(gu, gu_hbm, 6)
    ring_send("m", 2)
    ring_send("t", 2)
    tile_up(hb, htile)
    retile(gflat, z, gt)
    ring_send("m", 3)
    ring_send("t", 3)
    lax.fori_loop(0, 18, one_down, jnp.int32(0))
    store(gd, gd_hbm, 7)
    ring_end("m", ms2, mr2)
    ring_end("t", ts2, tr2)

    def finish(name, recv2, out):
        car, _, _, pos, cross, _, _ = outs[name]
        acc = car[pl.ds(pl.multiple_of(pos * 384 + cross * 48, 48), 48), :]
        for k, b in others:
            last[name, k, b].wait_recv()
            acc = acc + recv2[2 * k + b].astype(F32)
        rows4[...] = acc
        cols = [rows4[4 * r : 4 * r + 4, :] for r in range(12)]
        out[...] = jnp.concatenate(cols, axis=1).astype(BF)

    finish("m", mr2, mixed_out)
    finish("t", tr2, gt_out)
    drain(sent, stores)


N_COPIES = 14 + 56 + 8 + 12 + 56 + 56 + 14


def per_device(tokens, out_grad, up_tiles, down_tiles, up_slots, down_slots):
    vmem = pl.BlockSpec(memory_space=pltpu.VMEM)
    hbm = pl.BlockSpec(memory_space=pltpu.HBM)
    V = pltpu.VMEM
    return pl.pallas_call(
        kernel,
        out_shape=(
            jax.ShapeDtypeStruct((4, 1536), BF),
            jax.ShapeDtypeStruct((4, 1536), BF),
            jax.ShapeDtypeStruct((1, 1, 18, 128, 128), F32),
            jax.ShapeDtypeStruct((1, 1, 18, 128, 128), F32),
        ),
        in_specs=[hbm] * 6,
        out_specs=(vmem, vmem, hbm, hbm),
        scratch_shapes=[
            V((4, 1536), BF),
            V((4, 1536), BF),
            pltpu.SMEM((1, 1, 18), jnp.int32),
            pltpu.SMEM((1, 1, 18), jnp.int32),
            V((18, 128, 128), BF),
            V((18, 128, 128), BF),
            V((1536, 768), BF),
            V((768, 1536), BF),
            V((8, 8, 48, 128), BF),
            V((8, 8, 48, 128), BF),
            V((3072, 128), F32),
            V((3072, 128), F32),
            V((4, 64, 1536), BF),
            V((4, 64, 1536), BF),
            V((12, 256, 128), BF),
            V((12, 256, 128), BF),
            V((4, 2, 2, 64, 384), F32),
            V((4, 2, 64, 384), F32),
            V((4, 4, 2, 16, 384), BF),
            V((4, 4, 2, 16, 384), BF),
            V((4, 64, 768), BF),
            V((4, 64, 768), BF),
            V((3, 64, 128), F32),
            V((3, 64, 128), F32),
            V((6, 256, 128), BF),
            V((6, 256, 128), BF),
            V((3072, 128), F32),
            V((3072, 128), F32),
            V((2, 4, 384, 128), BF),
            V((2, 4, 384, 128), BF),
            V((2, 4, 384, 128), BF),
            V((2, 4, 384, 128), BF),
            V((384, 128), BF),
            V((8, 48, 128), BF),
            V((384, 128), BF),
            V((8, 48, 128), BF),
            V((48, 128), F32),
            V((18, 128, 128), F32),
            V((18, 128, 128), F32),
            pltpu.SemaphoreType.DMA((N_COPIES,)),
            pltpu.SemaphoreType.DMA((N_COPIES,)),
            pltpu.SemaphoreType.DMA((8,)),
        ],
        compiler_params=pltpu.CompilerParams(
            collective_id=0, has_side_effects=True, vmem_limit_bytes=56 * 1024 * 1024
        ),
    )(tokens, out_grad, up_tiles, down_tiles, up_slots, down_slots)


def solution(mesh):
    spec2, spec5, spec3 = P("hid", "wid"), P("hid", "wid", None, None, None), P("hid", "wid", None)
    return jax.shard_map(
        per_device,
        mesh=mesh,
        in_specs=(spec2, spec2, spec5, spec5, spec3, spec3),
        out_specs=(spec2, spec2, spec5, spec5),
        check_vma=False,
    )
```

```python
import functools

import jax
import jax.numpy as jnp
from jax import lax
from jax.experimental import pallas as pl
from jax.experimental.pallas import tpu as pltpu
from jax.sharding import PartitionSpec as P

MESH = pl.DeviceIdType.MESH
BF = jnp.bfloat16
F32 = jnp.float32

ROOT = 0.7978845608028654
CUBIC = 0.044715

NEAR = (0, 1, 3, 2)
FAR = (2, 3, 1, 0)


def gelu_both(v):
    inner = jnp.tanh(ROOT * (v + CUBIC * v * v * v))
    value = 0.5 * v * (1.0 + inner)
    slope = 0.5 * (1.0 + inner) + 0.5 * v * (1.0 - inner * inner) * ROOT * (
        1.0 + 3.0 * CUBIC * v * v
    )
    return value, slope


def up8(v):
    return lax.rem(v + 16, 8)


def drain(sent, stores):
    for cp in sent:
        cp.wait_send()
    for cp in stores:
        cp.wait()


def write_out(a, b, c, d, oa, ob, oc, od, sem):
    copies = [
        pltpu.make_async_copy(src, dst, sem.at[n])
        for n, (src, dst) in enumerate(((a, oa), (b, ob), (c, oc), (d, od)))
    ]
    for cp in copies:
        cp.start()
    for cp in copies:
        cp.wait()


def kernel(
    x_hbm, g_hbm, ut_hbm, dt_hbm, us_hbm, ds_hbm,
    mixed_out, gt_out, gu, gd,
    x_in, g_in, us, ds, ut, dt, w1, w2, xcar, gcar, xflat, gflat, xs, gs, xt, gt,
    part, rcore, sb, rx, hb, db, slopes, backs, htile, dtile,
    mcar, tcar, msend, mrecv, tsend, trecv, ms2, mr2, ts2, tr2, rows4,
    ssem, rsem, lsem,
):
    hid, wid = lax.axis_index("hid"), lax.axis_index("wid")
    z, y = lax.div(hid, 8), lax.rem(hid, 8)
    xx, c = lax.div(wid, 2), lax.rem(wid, 2)

    def at(zz, yy):
        return (up8(zz) * 8 + up8(yy), wid)

    def pair(pos, k):
        q = lax.div(pos, 2)
        return (q, q + 1 - 2 * lax.rem(q, 2), lax.rem(q + 2, 4), 3 - q)[k]

    def mate(pos, k, b):
        low = lax.rem(pos, 2)
        return pair(pos, k) * 2 + (1 - low if b else low)

    others = [(k, b) for k in NEAR for b in (0, 1) if (k, b) != (0, 0)]
    xpeer = [(hid, lax.rem(xx + o, 4) * 2 + c) for o in (1, 2, 3)]
    partner = (hid, xx * 2 + 1 - c)

    counter = [0]
    sent = []
    stores = []

    def rcopy(src, dst, dev):
        k = counter[0]
        counter[0] += 1
        cp = pltpu.make_async_remote_copy(
            src_ref=src, dst_ref=dst, send_sem=ssem.at[k], recv_sem=rsem.at[k],
            device_id=dev, device_id_type=MESH,
        )
        cp.start()
        sent.append(cp)
        return cp

    barrier = pltpu.get_barrier_semaphore()
    peers = [at(z, mate(y, k, b)) for k, b in others] + [at(mate(z, k, b), y) for k, b in others]
    peers += xpeer + [partner]
    for dev in peers:
        pl.semaphore_signal(barrier, inc=1, device_id=dev, device_id_type=MESH)

    loads = [
        pltpu.make_async_copy(a, b, lsem.at[n])
        for n, (a, b) in enumerate(
            (
                (x_hbm, x_in), (g_hbm, g_in), (us_hbm, us), (ds_hbm, ds),
                (ut_hbm.at[0, 0], ut), (dt_hbm.at[0, 0], dt),
            )
        )
    ]
    for cp in loads:
        cp.start()

    def to_rows(src, dst):
        val = src[...].astype(F32)
        for r in range(12):
            rows4[4 * r : 4 * r + 4, :] = val[:, r * 128 : (r + 1) * 128]
        dst[...] = rows4[...].astype(BF)

    loads[0].wait()
    to_rows(x_in, xcar.at[z, y])
    loads[1].wait()
    to_rows(g_in, gcar.at[y, z])
    pl.semaphore_wait(barrier, len(peers))

    first = {}
    for k, b in others:
        first["x", k, b] = rcopy(xcar.at[z, y], xcar.at[z, y], at(z, mate(y, k, b)))
        first["g", k, b] = rcopy(gcar.at[y, z], gcar.at[y, z], at(mate(z, k, b), y))

    for cp in loads[2:]:
        cp.wait()

    def build(slots, tiles, dense, rows, cols):
        def one(row, carry):
            pos = jnp.int32(0)
            for n in range(18):
                pos = pos + (slots[0, 0, n] < row * cols).astype(jnp.int32)
            for col in range(cols):
                idx = jnp.minimum(pos, 17)
                hit = jnp.logical_and(pos < 18, slots[0, 0, idx] == row * cols + col)
                tile = tiles[idx]
                dense[
                    pl.ds(pl.multiple_of(row * 128, 128), 128), col * 128 : (col + 1) * 128
                ] = jnp.where(hit, tile, jnp.zeros_like(tile))
                pos = pos + hit.astype(jnp.int32)
            return carry

        lax.fori_loop(0, rows, one, jnp.int32(0))

    build(us, ut, w1, 12, 6)
    build(ds, dt, w2, 6, 12)

    axes = {
        "x": (xcar, z, y, at(z + 1, y), at(z - 1, y)),
        "g": (gcar, y, z, at(z, y + 1), at(z, y - 1)),
    }
    ring = {}

    def offsets(g):
        return (-g, g + 1)

    def run(tasks, share):
        for _ in range(min(len(tasks), share)):
            tasks.pop(0)()

    def step(s, tasks=()):
        tasks = list(tasks)
        share = -(-len(tasks) // 5)
        run(tasks, share)
        for k in NEAR:
            for name in ("x", "g"):
                car, pos, cross, right, left = axes[name]
                if s == 0:
                    for b in (0, 1):
                        if (k, b) != (0, 0):
                            first[name, k, b].wait_recv()
                else:
                    ring[name, s - 1, k, "r"].wait_recv()
                    if s < 4:
                        ring[name, s - 1, k, "l"].wait_recv()
                span = pl.ds(pair(cross, k) * 2, 2)
                if s < 4:
                    ref = car.at[up8(pos - s), span]
                    ring[name, s, k, "r"] = rcopy(ref, ref, right)
                if s < 3:
                    ref = car.at[up8(pos + s), span]
                    ring[name, s, k, "l"] = rcopy(ref, ref, left)
            run(tasks, share)

    def widen(car, pos, flat, off):
        d = up8(pos + off)
        flat[pl.ds(pl.multiple_of(d * 384, 384), 384), :] = car[d].reshape(384, 128).astype(F32)

    def unpack(pos, flat, dst, g, tiles):
        for r in tiles:
            for i in range(4):
                rows = [
                    flat[pl.ds(up8(pos + off) * 384 + 4 * r + i, 8, stride=48), :]
                    for off in offsets(g)
                ]
                dst[g, i * 16 : (i + 1) * 16, r * 128 : (r + 1) * 128] = jnp.concatenate(
                    rows, axis=0
                ).astype(BF)

    core = {}
    over = {}
    back_home = {}

    def product(a, g, q):
        cols = slice(q * 256, (q + 1) * 256)
        if a == 0:
            val = jnp.dot(xs[g], w1[:, cols], preferred_element_type=F32)
        else:
            val = lax.dot_general(
                gs[g], w2[cols, :], (((1,), (1,)), ((), ())), preferred_element_type=F32
            )
        for t in range(2):
            n = 2 * q + t
            part[g, n // 3, a, :, (n % 3) * 128 : (n % 3 + 1) * 128] = val[
                :, t * 128 : (t + 1) * 128
            ]
        if q == 2:
            core[g, a] = rcopy(part.at[g, 1 - c, a], rcore.at[g, a], partner)

    def compute(g):
        tasks = []
        for a, car, pos, flat, dst in ((0, xcar, z, xflat, xs), (1, gcar, y, gflat, gs)):
            for off in offsets(g):
                tasks.append(functools.partial(widen, car, pos, flat, off))
            for t in range(4):
                tasks.append(functools.partial(unpack, pos, flat, dst, g, (3 * t, 3 * t + 1, 3 * t + 2)))
            for q in range(3):
                tasks.append(functools.partial(product, a, g, q))
        return tasks

    def sum_cores(g):
        for a in range(2):
            core[g, a].wait_recv()
            total = part[g, c, a] + rcore[g, a]
            rcore[g, a] = total
            for i in range(4):
                sb[g, i, a] = total[i * 16 : (i + 1) * 16].astype(BF)
        for dev, o in zip(xpeer, (1, 2, 3)):
            over[g, o] = rcopy(sb.at[g, lax.rem(xx + o, 4)], rx.at[g, o], dev)

    def mine(buf, g, i):
        return buf.at[
            g,
            pl.ds(pl.multiple_of(i * 16, 16), 16),
            pl.ds(pl.multiple_of(c * 384, 128), 384),
        ]

    def send_home(buf, name, g):
        ref = mine(buf, g, xx)
        back_home[name, g] = [rcopy(ref, ref, dev) for dev in xpeer] + [rcopy(ref, ref, partner)]

    def relay(buf, name, g):
        for n, o in enumerate((1, 2, 3)):
            back_home[name, g][n].wait_recv()
            ref = mine(buf, g, lax.rem(xx + 4 - o, 4))
            back_home[name, g].append(rcopy(ref, ref, partner))

    def all_home(name, g):
        for cp in back_home[name, g][3:]:
            cp.wait_recv()

    def sum_chips(g):
        acc = [rcore[g, a, pl.ds(pl.multiple_of(xx * 16, 16), 16), :] for a in range(2)]
        for o in (1, 2, 3):
            over[g, o].wait_recv()
            acc = [acc[a] + rx[g, o, a].astype(F32) for a in range(2)]
        value, slope = gelu_both(acc[0])
        ref = mine(hb, g, xx)
        ref[...] = value.astype(BF)
        send_home(hb, "h", g)
        for n, off in enumerate(offsets(g)):
            dz, dy = up8(z + off), up8(y + off)
            for t in range(3):
                lanes = slice(t * 128, (t + 1) * 128)
                slopes[t, pl.ds(pl.multiple_of(dz * 8, 8), 8), :] = slope[
                    n * 8 : (n + 1) * 8, lanes
                ]
                backs[t, pl.ds(pl.multiple_of(dy * 8, 8), 8), :] = acc[1][
                    n * 8 : (n + 1) * 8, lanes
                ]

    def delta(g):
        rows = []
        for off in offsets(g):
            dy = up8(y + off)
            rows.append(
                jnp.concatenate(
                    [
                        backs[t, pl.ds(pl.multiple_of(dy * 8, 8), 8), :]
                        * slopes[t, pl.ds(dy, 8, stride=8), :]
                        for t in range(3)
                    ],
                    axis=1,
                )
            )
        ref = mine(db, g, xx)
        ref[...] = jnp.concatenate(rows, axis=0).astype(BF)
        send_home(db, "d", g)

    def retile(flat, pos, dst):
        def one(g, carry):
            for r in range(12):
                for i in range(4):
                    rows = [
                        flat[pl.ds(up8(pos - g + n * (2 * g + 1)) * 48 + 4 * r + i, 8, stride=384), :]
                        for n in range(2)
                    ]
                    dst[r, pl.ds(pl.multiple_of(g * 64 + i * 16, 16), 16), :] = jnp.concatenate(
                        rows, axis=0
                    ).astype(BF)
            return carry

        lax.fori_loop(0, 4, one, jnp.int32(0))

    def pack(val, r, car, pos, groups):
        for n, g in enumerate(groups):
            for i in range(4):
                for m, off in enumerate(offsets(g)):
                    lo = n * 64 + i * 16 + m * 8
                    car[pl.ds(up8(pos + off) * 384 + 4 * r + i, 8, stride=48), :] = val[lo : lo + 8]

    def mixed_part(groups):
        lhs = jnp.concatenate([hb[g] for g in groups], axis=0)

        def cols(q, carry):
            val = jnp.dot(
                lhs, w2[:, pl.ds(pl.multiple_of(q * 256, 256), 256)], preferred_element_type=F32
            )
            pack(val[:, :128], 2 * q, mcar, z, groups)
            pack(val[:, 128:], 2 * q + 1, mcar, z, groups)
            return carry

        lax.fori_loop(0, 6, cols, jnp.int32(0))

    def back_part(groups):
        lhs = jnp.concatenate([db[g] for g in groups], axis=0)

        def cols(q, carry):
            val = lax.dot_general(
                lhs,
                w1[pl.ds(pl.multiple_of(q * 256, 256), 256), :],
                (((1,), (1,)), ((), ())),
                preferred_element_type=F32,
            )
            pack(val[:, :128], 2 * q, tcar, y, groups)
            pack(val[:, 128:], 2 * q + 1, tcar, y, groups)
            return carry

        lax.fori_loop(0, 6, cols, jnp.int32(0))

    outs = {
        "m": (mcar, msend, mrecv, z, y, at(z + 1, y), at(z - 1, y)),
        "t": (tcar, tsend, trecv, y, z, at(z, y + 1), at(z, y - 1)),
    }
    rsum = {}

    def ring_send(name, s):
        car, send, recv, pos, cross, right, left = outs[name]
        for k in FAR:
            at_rows = pair(cross, k) * 96
            span = pl.ds(pl.multiple_of(at_rows, 96), 96)
            for w, dev, d in ((0, right, pos + 4 - s), (1, left, pos - 3 + s)):
                if w == 1 and s == 3:
                    continue
                val = car[pl.ds(pl.multiple_of(up8(d) * 384 + at_rows, 96), 96), :]
                if s > 0:
                    rsum[name, s - 1, k, w].wait_recv()
                    val = val + recv[w, s - 1, span, :].astype(F32)
                send[w, s, span, :] = val.astype(BF)
                rsum[name, s, k, w] = rcopy(
                    send.at[w, s, span, :], recv.at[w, s, span, :], dev
                )

    last = {}

    def ring_end(name, send2, recv2):
        car, send, recv, pos, cross, right, left = outs[name]
        for k in FAR:
            at_rows = pair(cross, k) * 96
            span = pl.ds(pl.multiple_of(at_rows, 96), 96)
            rsum[name, 3, k, 0].wait_recv()
            rsum[name, 2, k, 1].wait_recv()
            here = pl.ds(pl.multiple_of(pos * 384 + at_rows, 96), 96)
            val = car[here, :] + recv[0, 3, span, :].astype(F32) + recv[1, 2, span, :].astype(F32)
            car[here, :] = val
            send2[span, :] = val.astype(BF)
            for b in (0, 1):
                if (k, b) == (0, 0):
                    continue
                to = mate(cross, k, b)
                dev = at(pos, to) if name == "m" else at(to, pos)
                n = 2 * k + b
                last[name, k, b] = rcopy(
                    send2.at[pl.ds(pl.multiple_of(to * 48, 48), 48), :], recv2.at[n], dev
                )

    def up_some(lo, hi):
        def one(n, carry):
            slot = us[0, 0, n]
            lhs, rhs = xt[lax.div(slot, 6)], dtile[lax.rem(slot, 6)]
            gu[0, 0, n] = lax.dot_general(
                lhs, rhs, (((0,), (0,)), ((), ())), preferred_element_type=F32
            )
            return carry

        lax.fori_loop(lo, hi, one, jnp.int32(0))

    def down_some(lo, hi):
        def one(n, carry):
            slot = ds[0, 0, n]
            lhs, rhs = htile[lax.div(slot, 12)], gt[lax.rem(slot, 12)]
            gd[0, 0, n] = lax.dot_general(
                lhs, rhs, (((0,), (0,)), ((), ())), preferred_element_type=F32
            )
            return carry

        lax.fori_loop(lo, hi, one, jnp.int32(0))

    def tile_up(buf, dst):
        for b in range(6):
            dst[b] = buf[:, :, b * 128 : (b + 1) * 128].reshape(256, 128)

    P_ = functools.partial
    step(0)
    step(1)
    step(2, compute(0))
    step(3, [P_(sum_cores, 0)] + compute(1))
    step(4, [P_(sum_cores, 1), P_(sum_chips, 0)] + compute(2) + [P_(sum_cores, 2)])
    for task in compute(3):
        task()
    sum_chips(1)
    sum_cores(3)
    relay(hb, "h", 0)
    retile(xflat, y, xt)
    sum_chips(2)
    relay(hb, "h", 1)
    retile(gflat, z, gt)
    sum_chips(3)
    for g in (3, 2, 1, 0):
        delta(g)
    relay(hb, "h", 2)
    for g in (0, 1, 2):
        all_home("h", g)
    mixed_part((0, 1, 2))
    relay(hb, "h", 3)
    relay(db, "d", 3)
    all_home("h", 3)
    mixed_part((3,))
    ring_send("m", 0)
    all_home("d", 3)
    back_part((3,))
    ring_send("t", 0)
    relay(db, "d", 2)
    relay(db, "d", 1)
    relay(db, "d", 0)
    all_home("d", 2)
    back_part((2,))
    ring_send("m", 1)
    ring_send("t", 1)
    all_home("d", 1)
    all_home("d", 0)
    back_part((1, 0))
    ring_send("m", 2)
    ring_send("t", 2)
    tile_up(db, dtile)
    tile_up(hb, htile)
    up_some(0, 9)
    ring_send("m", 3)
    ring_send("t", 3)
    up_some(9, 18)
    ring_end("m", ms2, mr2)
    ring_end("t", ts2, tr2)
    down_some(0, 18)

    def finish(name, recv2, out):
        car, _, _, pos, cross, _, _ = outs[name]
        acc = car[pl.ds(pl.multiple_of(pos * 384 + cross * 48, 48), 48), :]
        for k, b in others:
            last[name, k, b].wait_recv()
            acc = acc + recv2[2 * k + b].astype(F32)
        rows4[...] = acc
        cols = [rows4[4 * r : 4 * r + 4, :] for r in range(12)]
        out[...] = jnp.concatenate(cols, axis=1).astype(BF)

    finish("m", mr2, mixed_out)
    finish("t", tr2, gt_out)
    drain(sent, stores)


N_COPIES = 14 + 56 + 8 + 12 + 56 + 56 + 14


def per_device(tokens, out_grad, up_tiles, down_tiles, up_slots, down_slots):
    vmem = pl.BlockSpec(memory_space=pltpu.VMEM)
    hbm = pl.BlockSpec(memory_space=pltpu.HBM)
    V = pltpu.VMEM
    results = pl.pallas_call(
        kernel,
        out_shape=(
            V((4, 1536), BF),
            V((4, 1536), BF),
            V((1, 1, 18, 128, 128), F32),
            V((1, 1, 18, 128, 128), F32),
        ),
        in_specs=[hbm] * 6,
        out_specs=(vmem,) * 4,
        scratch_shapes=[
            V((4, 1536), BF),
            V((4, 1536), BF),
            pltpu.SMEM((1, 1, 18), jnp.int32),
            pltpu.SMEM((1, 1, 18), jnp.int32),
            V((18, 128, 128), BF),
            V((18, 128, 128), BF),
            V((1536, 768), BF),
            V((768, 1536), BF),
            V((8, 8, 48, 128), BF),
            V((8, 8, 48, 128), BF),
            V((3072, 128), F32),
            V((3072, 128), F32),
            V((4, 64, 1536), BF),
            V((4, 64, 1536), BF),
            V((12, 256, 128), BF),
            V((12, 256, 128), BF),
            V((4, 2, 2, 64, 384), F32),
            V((4, 2, 64, 384), F32),
            V((4, 4, 2, 16, 384), BF),
            V((4, 4, 2, 16, 384), BF),
            V((4, 64, 768), BF),
            V((4, 64, 768), BF),
            V((3, 64, 128), F32),
            V((3, 64, 128), F32),
            V((6, 256, 128), BF),
            V((6, 256, 128), BF),
            V((3072, 128), F32),
            V((3072, 128), F32),
            V((2, 4, 384, 128), BF),
            V((2, 4, 384, 128), BF),
            V((2, 4, 384, 128), BF),
            V((2, 4, 384, 128), BF),
            V((384, 128), BF),
            V((8, 48, 128), BF),
            V((384, 128), BF),
            V((8, 48, 128), BF),
            V((48, 128), F32),
            pltpu.SemaphoreType.DMA((N_COPIES,)),
            pltpu.SemaphoreType.DMA((N_COPIES,)),
            pltpu.SemaphoreType.DMA((8,)),
        ],
        compiler_params=pltpu.CompilerParams(
            collective_id=0, has_side_effects=True, vmem_limit_bytes=40 * 1024 * 1024
        ),
    )(
        *(
            pltpu.with_memory_space_constraint(a, pltpu.HBM)
            for a in (tokens, out_grad, up_tiles, down_tiles, up_slots, down_slots)
        )
    )
    return pl.pallas_call(
        write_out,
        out_shape=tuple(jax.ShapeDtypeStruct(r.shape, r.dtype) for r in results),
        in_specs=[vmem] * 4,
        out_specs=(hbm,) * 4,
        scratch_shapes=[pltpu.SemaphoreType.DMA((4,))],
    )(*results)


def solution(mesh):
    spec2, spec5, spec3 = P("hid", "wid"), P("hid", "wid", None, None, None), P("hid", "wid", None)
    return jax.shard_map(
        per_device,
        mesh=mesh,
        in_specs=(spec2, spec2, spec5, spec5, spec3, spec3),
        out_specs=(spec2, spec2, spec5, spec5),
        check_vma=False,
    )
```

```python
import functools

import jax
import jax.numpy as jnp
from jax import lax
from jax.experimental import pallas as pl
from jax.experimental.pallas import tpu as pltpu
from jax.sharding import PartitionSpec as P

MESH = pl.DeviceIdType.MESH
BF = jnp.bfloat16
F32 = jnp.float32

ROOT = 0.7978845608028654
CUBIC = 0.044715

NEAR = (0, 1, 3, 2)
FAR = (2, 3, 1, 0)
ORDER = FAR
SKIP = (2, 3)
REACH = ((4, 3), (3, 4), (3, 3), (3, 3))
SHORT = ()
SUMS = ((4, 3),) * 4


def gelu_both(v):
    inner = jnp.tanh(ROOT * (v + CUBIC * v * v * v))
    value = 0.5 * v * (1.0 + inner)
    slope = 0.5 * (1.0 + inner) + 0.5 * v * (1.0 - inner * inner) * ROOT * (
        1.0 + 3.0 * CUBIC * v * v
    )
    return value, slope


def up8(v):
    return lax.rem(v + 16, 8)


def drain(sent, stores):
    for cp in sent:
        cp.wait_send()
    for cp in stores:
        cp.wait()


def write_out(a, b, c, d, oa, ob, oc, od, sem):
    copies = [
        pltpu.make_async_copy(src, dst, sem.at[n])
        for n, (src, dst) in enumerate(((a, oa), (b, ob), (c, oc), (d, od)))
    ]
    for cp in copies:
        cp.start()
    for cp in copies:
        cp.wait()


def kernel(
    x_hbm, g_hbm, ut_hbm, dt_hbm, us_hbm, ds_hbm,
    mixed_out, gt_out, gu, gd,
    x_in, g_in, us, ds, ut, dt, w1, w2, xcar, gcar, xflat, gflat, xs, gs, xt, gt,
    part, rcore, sb, rx, hb, db, slopes, backs, htile, dtile,
    mcar, tcar, msend, mrecv, tsend, trecv, ms2, mr2, ts2, tr2, rows4,
    ssem, rsem, lsem,
):
    hid, wid = lax.axis_index("hid"), lax.axis_index("wid")
    z, y = lax.div(hid, 8), lax.rem(hid, 8)
    xx, c = lax.div(wid, 2), lax.rem(wid, 2)

    def at(zz, yy):
        return (up8(zz) * 8 + up8(yy), wid)

    def pair(pos, k):
        q = lax.div(pos, 2)
        return (q, q + 1 - 2 * lax.rem(q, 2), lax.rem(q + 2, 4), 3 - q)[k]

    def mate(pos, k, b):
        low = lax.rem(pos, 2)
        return pair(pos, k) * 2 + (1 - low if b else low)

    others = [(k, b) for k in FAR for b in (0, 1) if (k, b) != (0, 0)]
    xpeer = [(hid, lax.rem(xx + o, 4) * 2 + c) for o in (1, 2, 3)]
    xcross = [(hid, lax.rem(xx + o, 4) * 2 + 1 - c) for o in (1, 2, 3)]
    partner = (hid, xx * 2 + 1 - c)

    counter = [0]
    sent = []
    stores = []

    def rcopy(src, dst, dev):
        k = counter[0]
        counter[0] += 1
        cp = pltpu.make_async_remote_copy(
            src_ref=src, dst_ref=dst, send_sem=ssem.at[k], recv_sem=rsem.at[k],
            device_id=dev, device_id_type=MESH,
        )
        cp.start()
        sent.append(cp)
        return cp

    barrier = pltpu.get_barrier_semaphore()
    peers = [at(z, mate(y, k, b)) for k, b in others] + [at(mate(z, k, b), y) for k, b in others]
    peers += xpeer + xcross + [partner]
    for dev in peers:
        pl.semaphore_signal(barrier, inc=1, device_id=dev, device_id_type=MESH)

    loads = [
        pltpu.make_async_copy(a, b, lsem.at[n])
        for n, (a, b) in enumerate(
            (
                (x_hbm, x_in), (g_hbm, g_in), (us_hbm, us), (ds_hbm, ds),
                (ut_hbm.at[0, 0], ut), (dt_hbm.at[0, 0], dt),
            )
        )
    ]
    for cp in loads:
        cp.start()

    def to_rows(src, dst):
        val = src[...].astype(F32)
        for r in range(12):
            rows4[4 * r : 4 * r + 4, :] = val[:, r * 128 : (r + 1) * 128]
        dst[...] = rows4[...].astype(BF)

    loads[0].wait()
    to_rows(x_in, xcar.at[z, y])
    loads[1].wait()
    to_rows(g_in, gcar.at[y, z])
    pl.semaphore_wait(barrier, len(peers))

    first = {}
    for k, b in others:
        first["x", k, b] = rcopy(xcar.at[z, y], xcar.at[z, y], at(z, mate(y, k, b)))
        first["g", k, b] = rcopy(gcar.at[y, z], gcar.at[y, z], at(mate(z, k, b), y))

    for cp in loads[2:]:
        cp.wait()

    def build(slots, tiles, dense, rows, cols):
        def one(row, carry):
            pos = jnp.int32(0)
            for n in range(18):
                pos = pos + (slots[0, 0, n] < row * cols).astype(jnp.int32)
            for col in range(cols):
                idx = jnp.minimum(pos, 17)
                hit = jnp.logical_and(pos < 18, slots[0, 0, idx] == row * cols + col)
                tile = tiles[idx]
                dense[
                    pl.ds(pl.multiple_of(row * 128, 128), 128), col * 128 : (col + 1) * 128
                ] = jnp.where(hit, tile, jnp.zeros_like(tile))
                pos = pos + hit.astype(jnp.int32)
            return carry

        lax.fori_loop(0, rows, one, jnp.int32(0))

    build(us, ut, w1, 12, 6)
    build(ds, dt, w2, 6, 12)

    axes = {
        "x": (xcar, z, y, lambda d: at(z + d, y)),
        "g": (gcar, y, z, lambda d: at(z, y + d)),
    }
    ring = {}

    def offsets(g):
        return (-g, g + 1)

    def run(tasks, share):
        for _ in range(min(len(tasks), share)):
            tasks.pop(0)()

    def step(s, tasks=()):
        tasks = list(tasks)
        share = -(-len(tasks) // 5)
        run(tasks, share)
        for k in NEAR:
            for name in ("x", "g"):
                car, pos, cross, dev = axes[name]
                span = pl.ds(pair(cross, k) * 2, 2)

                def forward(slab, hops, key):
                    ref = car.at[up8(slab), span]
                    ring[(name, k) + key] = rcopy(ref, ref, dev(hops))

                if s == 0:
                    for b in (0, 1):
                        if (k, b) != (0, 0):
                            first[name, k, b].wait_recv()
                else:
                    for way in (0, 1):
                        if s <= REACH[k][way]:
                            ring[name, k, s - 1, way].wait_recv()
                    if s == 4 and k in SKIP:
                        ring[name, k, 2, 2].wait_recv()
                if s == 2 and k in SKIP:
                    way = 1 if k == 2 else -1
                    forward(pos - 2 * way, 2 * way, (2, 2))
                for way in (0, 1):
                    if s < REACH[k][way]:
                        sign = 1 - 2 * way
                        forward(pos - sign * s, sign, (s, way))
            run(tasks, share)

    def widen(car, pos, flat, off):
        d = up8(pos + off)
        flat[pl.ds(pl.multiple_of(d * 384, 384), 384), :] = car[d].reshape(384, 128).astype(F32)

    def unpack(pos, flat, dst, g, tiles):
        for r in tiles:
            for i in range(4):
                rows = [
                    flat[pl.ds(up8(pos + off) * 384 + 4 * r + i, 8, stride=48), :]
                    for off in offsets(g)
                ]
                dst[g, i * 16 : (i + 1) * 16, r * 128 : (r + 1) * 128] = jnp.concatenate(
                    rows, axis=0
                ).astype(BF)

    core = {}
    over = {}
    back_home = {}

    def product(a, g, q):
        cols = slice(q * 256, (q + 1) * 256)
        if a == 0:
            val = jnp.dot(xs[g], w1[:, cols], preferred_element_type=F32)
        else:
            val = lax.dot_general(
                gs[g], w2[cols, :], (((1,), (1,)), ((), ())), preferred_element_type=F32
            )
        for t in range(2):
            n = 2 * q + t
            part[g, n // 3, a, :, (n % 3) * 128 : (n % 3 + 1) * 128] = val[
                :, t * 128 : (t + 1) * 128
            ]
        if q == 2:
            core[g, a] = rcopy(part.at[g, 1 - c, a], rcore.at[g, a], partner)

    def compute(g, a):
        car, pos, flat, dst = ((xcar, z, xflat, xs), (gcar, y, gflat, gs))[a]
        tasks = [functools.partial(widen, car, pos, flat, off) for off in offsets(g)]
        for t in range(4):
            tasks.append(
                functools.partial(unpack, pos, flat, dst, g, (3 * t, 3 * t + 1, 3 * t + 2))
            )
        return tasks + [functools.partial(product, a, g, q) for q in range(3)]

    def compute_now(g, a):
        for task in compute(g, a):
            task()

    def sum_cores(g, a):
        core[g, a].wait_recv()
        total = part[g, c, a] + rcore[g, a]
        rcore[g, a] = total
        for i in range(4):
            sb[g, i, a] = total[i * 16 : (i + 1) * 16].astype(BF)
        for dev, o in zip(xpeer, (1, 2, 3)):
            over[g, a, o] = rcopy(sb.at[g, lax.rem(xx + o, 4), a], rx.at[g, o, a], dev)

    def mine(buf, g, i):
        return buf.at[
            g,
            pl.ds(pl.multiple_of(i * 16, 16), 16),
            pl.ds(pl.multiple_of(c * 384, 128), 384),
        ]

    def send_home(buf, name, g):
        ref = mine(buf, g, xx)
        devs = xpeer + [partner] + (xcross if g == 3 else [])
        back_home[name, g] = [rcopy(ref, ref, dev) for dev in devs]

    def relay(buf, name, g):
        for n, o in enumerate((1, 2, 3)):
            back_home[name, g][n].wait_recv()
            ref = mine(buf, g, lax.rem(xx + 4 - o, 4))
            back_home[name, g].append(rcopy(ref, ref, partner))

    def all_home(name, g):
        for cp in back_home[name, g][0 if g == 3 else 3 :]:
            cp.wait_recv()

    def sum_chips(g, a):
        acc = rcore[g, a, pl.ds(pl.multiple_of(xx * 16, 16), 16), :]
        for o in (1, 2, 3):
            over[g, a, o].wait_recv()
            acc = acc + rx[g, o, a].astype(F32)
        return acc

    def lay(buf, val, pos, g):
        for n, off in enumerate(offsets(g)):
            d = up8(pos + off)
            for t in range(3):
                buf[t, pl.ds(pl.multiple_of(d * 8, 8), 8), :] = val[
                    n * 8 : (n + 1) * 8, t * 128 : (t + 1) * 128
                ]

    def hidden(g):
        value, slope = gelu_both(sum_chips(g, 0))
        ref = mine(hb, g, xx)
        ref[...] = value.astype(BF)
        send_home(hb, "h", g)
        lay(slopes, slope, z, g)

    def delta(g):
        lay(backs, sum_chips(g, 1), y, g)
        rows = []
        for off in offsets(g):
            dy = up8(y + off)
            rows.append(
                jnp.concatenate(
                    [
                        backs[t, pl.ds(pl.multiple_of(dy * 8, 8), 8), :]
                        * slopes[t, pl.ds(dy, 8, stride=8), :]
                        for t in range(3)
                    ],
                    axis=1,
                )
            )
        ref = mine(db, g, xx)
        ref[...] = jnp.concatenate(rows, axis=0).astype(BF)
        send_home(db, "d", g)

    def retile(flat, pos, dst):
        def one(g, carry):
            for r in range(12):
                for i in range(4):
                    rows = [
                        flat[pl.ds(up8(pos - g + n * (2 * g + 1)) * 48 + 4 * r + i, 8, stride=384), :]
                        for n in range(2)
                    ]
                    dst[r, pl.ds(pl.multiple_of(g * 64 + i * 16, 16), 16), :] = jnp.concatenate(
                        rows, axis=0
                    ).astype(BF)
            return carry

        lax.fori_loop(0, 4, one, jnp.int32(0))

    def pack(val, r, car, pos, groups):
        for n, g in enumerate(groups):
            for i in range(4):
                for m, off in enumerate(offsets(g)):
                    lo = n * 64 + i * 16 + m * 8
                    car[pl.ds(up8(pos + off) * 384 + 4 * r + i, 8, stride=48), :] = val[lo : lo + 8]

    def mixed_part(groups):
        lhs = jnp.concatenate([hb[g] for g in groups], axis=0)

        def cols(q, carry):
            val = jnp.dot(
                lhs, w2[:, pl.ds(pl.multiple_of(q * 256, 256), 256)], preferred_element_type=F32
            )
            pack(val[:, :128], 2 * q, mcar, z, groups)
            pack(val[:, 128:], 2 * q + 1, mcar, z, groups)
            return carry

        for q in range(6):
            cols(q, 0)

    def back_part(groups):
        lhs = jnp.concatenate([db[g] for g in groups], axis=0)

        def cols(q, carry):
            val = lax.dot_general(
                lhs,
                w1[pl.ds(pl.multiple_of(q * 256, 256), 256), :],
                (((1,), (1,)), ((), ())),
                preferred_element_type=F32,
            )
            pack(val[:, :128], 2 * q, tcar, y, groups)
            pack(val[:, 128:], 2 * q + 1, tcar, y, groups)
            return carry

        for q in range(6):
            cols(q, 0)

    outs = {
        "m": (mcar, msend, mrecv, z, y, lambda d: at(z + d, y), ms2, mr2),
        "t": (tcar, tsend, trecv, y, z, lambda d: at(z, y + d), ts2, tr2),
    }
    rsum = {}
    last = {}

    def block(name, k, d):
        car, pos, cross = outs[name][0], outs[name][3], outs[name][4]
        return pl.ds(pl.multiple_of(up8(pos + d) * 384 + pair(cross, k) * 96, 96), 96)

    def span_of(name, k):
        return pl.ds(pl.multiple_of(pair(outs[name][4], k) * 96, 96), 96)

    def got(name, k, way, s):
        rsum[name, k, way, s].wait_recv()
        return outs[name][2][way, s, span_of(name, k), :].astype(F32)

    def ring_send(name, k, s):
        car, send, recv, pos, cross, dev, _, _ = outs[name]
        span = span_of(name, k)

        def push(val, way, hops):
            send[way, s, span, :] = val.astype(BF)
            rsum[name, k, way, s] = rcopy(
                send.at[way, s, span, :], recv.at[way, s, span, :], dev(hops)
            )

        far_way = SHORT.index(k) if k in SHORT else None
        if s == 0 and k in SHORT:
            push(car[block(name, k, 4), :], 2, 2 - 4 * far_way)
        for way in (0, 1):
            reach = SUMS[k][way] - s
            if reach < 1:
                continue
            val = car[block(name, k, reach if way == 0 else -reach), :]
            if s > 0:
                val = val + got(name, k, way, s - 1)
            if s == 1 and far_way == way:
                val = val + got(name, k, 2, 0)
            push(val, way, 1 - 2 * way)

    def ring_end(name, k):
        car, _, _, pos, cross, _, send2, recv2 = outs[name]
        span = span_of(name, k)
        here = block(name, k, 0)
        val = car[here, :] + got(name, k, 0, SUMS[k][0] - 1) + got(name, k, 1, SUMS[k][1] - 1)
        car[here, :] = val
        send2[span, :] = val.astype(BF)
        for b in (0, 1):
            if (k, b) == (0, 0):
                continue
            to = mate(cross, k, b)
            dev = at(pos, to) if name == "m" else at(to, pos)
            last[name, k, b] = rcopy(
                send2.at[pl.ds(pl.multiple_of(to * 48, 48), 48), :], recv2.at[2 * k + b], dev
            )

    def ring_step(s, names=("m", "t"), pairs=ORDER, tasks=()):
        tasks = list(tasks)
        share = -(-len(tasks) // len(pairs))
        for k in pairs:
            for name in names:
                if s == 3 and k in SHORT:
                    ring_end(name, k)
                elif s == 4:
                    ring_end(name, k)
                else:
                    ring_send(name, k, s)
            run(tasks, share)

    def up_some(lo, hi):
        def one(n):
            slot = us[0, 0, n]
            lhs, rhs = xt[lax.div(slot, 6)], dtile[lax.rem(slot, 6)]
            gu[0, 0, n] = lax.dot_general(
                lhs, rhs, (((0,), (0,)), ((), ())), preferred_element_type=F32
            )

        def six(t, carry):
            for n in range(6):
                one(lo + 6 * t + n)
            return carry

        lax.fori_loop(0, (hi - lo) // 6, six, jnp.int32(0))

    def down_some(lo, hi):
        def one(n):
            slot = ds[0, 0, n]
            lhs, rhs = htile[lax.div(slot, 12)], gt[lax.rem(slot, 12)]
            gd[0, 0, n] = lax.dot_general(
                lhs, rhs, (((0,), (0,)), ((), ())), preferred_element_type=F32
            )

        def six(t, carry):
            for n in range(6):
                one(lo + 6 * t + n)
            return carry

        lax.fori_loop(0, (hi - lo) // 6, six, jnp.int32(0))

    def tile_up(buf, dst):
        for b in range(6):
            dst[b] = buf[:, :, b * 128 : (b + 1) * 128].reshape(256, 128)

    P_ = functools.partial
    step(0)
    step(1)
    step(2, compute(0, 0))
    todo = compute(1, 0)
    step(3, todo[:5] + [P_(sum_cores, 0, 0)] + todo[5:])
    todo = compute(2, 0)
    step(4, todo[:5] + [P_(sum_cores, 1, 0)] + todo[5:])
    compute_now(3, 0)
    sum_cores(2, 0)
    compute_now(3, 1)
    sum_cores(3, 0)
    compute_now(2, 1)
    sum_cores(3, 1)
    hidden(0)
    compute_now(1, 1)
    sum_cores(2, 1)
    hidden(1)
    compute_now(0, 1)
    sum_cores(1, 1)
    hidden(2)
    sum_cores(0, 1)
    relay(hb, "h", 0)
    hidden(3)
    delta(3)
    relay(hb, "h", 1)
    delta(2)
    retile(xflat, y, xt)
    delta(1)
    delta(0)
    relay(hb, "h", 2)
    all_home("h", 2)
    mixed_part((2,))
    all_home("h", 3)
    mixed_part((3,))
    ring_step(0, names=("m",))
    all_home("d", 3)
    back_part((3,))
    ring_step(0, names=("t",))
    relay(db, "d", 2)
    all_home("d", 2)
    back_part((2,))
    ring_step(1)
    relay(db, "d", 1)
    relay(db, "d", 0)
    for g in (1, 0):
        all_home("h", g)
        all_home("d", g)
    mixed_part((1, 0))
    back_part((1, 0))
    ring_step(2)
    tile_up(db, dtile)
    up_some(0, 6)
    ring_step(3)
    up_some(6, 18)
    ring_step(4)
    tile_up(hb, htile)
    retile(gflat, z, gt)
    down_some(0, 18)

    def finish(name, recv2, out):
        car, _, _, pos, cross, _, _, _ = outs[name]
        acc = car[pl.ds(pl.multiple_of(pos * 384 + cross * 48, 48), 48), :]
        for k, b in others:
            last[name, k, b].wait_recv()
            acc = acc + recv2[2 * k + b].astype(F32)
        rows4[...] = acc
        cols = [rows4[4 * r : 4 * r + 4, :] for r in range(12)]
        out[...] = jnp.concatenate(cols, axis=1).astype(BF)

    finish("m", mr2, mixed_out)
    finish("t", tr2, gt_out)
    drain(sent, stores)


N_COPIES = 14 + 56 + 8 + 24 + 56 + 56 + 14 + 16


def per_device(tokens, out_grad, up_tiles, down_tiles, up_slots, down_slots):
    vmem = pl.BlockSpec(memory_space=pltpu.VMEM)
    hbm = pl.BlockSpec(memory_space=pltpu.HBM)
    V = pltpu.VMEM
    results = pl.pallas_call(
        kernel,
        out_shape=(
            V((4, 1536), BF),
            V((4, 1536), BF),
            V((1, 1, 18, 128, 128), F32),
            V((1, 1, 18, 128, 128), F32),
        ),
        in_specs=[hbm] * 6,
        out_specs=(vmem,) * 4,
        scratch_shapes=[
            V((4, 1536), BF),
            V((4, 1536), BF),
            pltpu.SMEM((1, 1, 18), jnp.int32),
            pltpu.SMEM((1, 1, 18), jnp.int32),
            V((18, 128, 128), BF),
            V((18, 128, 128), BF),
            V((1536, 768), BF),
            V((768, 1536), BF),
            V((8, 8, 48, 128), BF),
            V((8, 8, 48, 128), BF),
            V((3072, 128), F32),
            V((3072, 128), F32),
            V((4, 64, 1536), BF),
            V((4, 64, 1536), BF),
            V((12, 256, 128), BF),
            V((12, 256, 128), BF),
            V((4, 2, 2, 64, 384), F32),
            V((4, 2, 64, 384), F32),
            V((4, 4, 2, 16, 384), BF),
            V((4, 4, 2, 16, 384), BF),
            V((4, 64, 768), BF),
            V((4, 64, 768), BF),
            V((3, 64, 128), F32),
            V((3, 64, 128), F32),
            V((6, 256, 128), BF),
            V((6, 256, 128), BF),
            V((3072, 128), F32),
            V((3072, 128), F32),
            V((3, 4, 384, 128), BF),
            V((3, 4, 384, 128), BF),
            V((3, 4, 384, 128), BF),
            V((3, 4, 384, 128), BF),
            V((384, 128), BF),
            V((8, 48, 128), BF),
            V((384, 128), BF),
            V((8, 48, 128), BF),
            V((48, 128), F32),
            pltpu.SemaphoreType.DMA((N_COPIES,)),
            pltpu.SemaphoreType.DMA((N_COPIES,)),
            pltpu.SemaphoreType.DMA((8,)),
        ],
        compiler_params=pltpu.CompilerParams(
            collective_id=0, has_side_effects=True, vmem_limit_bytes=40 * 1024 * 1024
        ),
    )(
        *(
            pltpu.with_memory_space_constraint(a, pltpu.HBM)
            for a in (tokens, out_grad, up_tiles, down_tiles, up_slots, down_slots)
        )
    )
    return pl.pallas_call(
        write_out,
        out_shape=tuple(jax.ShapeDtypeStruct(r.shape, r.dtype) for r in results),
        in_specs=[vmem] * 4,
        out_specs=(hbm,) * 4,
        scratch_shapes=[pltpu.SemaphoreType.DMA((4,))],
        compiler_params=pltpu.CompilerParams(vmem_limit_bytes=4 * 1024 * 1024),
    )(*(pltpu.with_memory_space_constraint(r, pltpu.VMEM) for r in results))


def solution(mesh):
    spec2, spec5, spec3 = P("hid", "wid"), P("hid", "wid", None, None, None), P("hid", "wid", None)
    return jax.shard_map(
        per_device,
        mesh=mesh,
        in_specs=(spec2, spec2, spec5, spec5, spec3, spec3),
        out_specs=(spec2, spec2, spec5, spec5),
        check_vma=False,
    )
```

```python
import functools

import jax
import jax.numpy as jnp
from jax import lax
from jax.experimental import pallas as pl
from jax.experimental.pallas import tpu as pltpu
from jax.sharding import PartitionSpec as P

MESH = pl.DeviceIdType.MESH
BF = jnp.bfloat16
F32 = jnp.float32

ROOT = 0.7978845608028654
CUBIC = 0.044715

NEAR = (0, 1, 3, 2)
FAR = (2, 3, 1, 0)
ORDER = FAR
SKIP = (2, 3)
REACH = ((4, 3), (3, 4), (3, 3), (3, 3))
SHORT = ()
SUMS = ((4, 3),) * 4


def gelu_both(v):
    inner = jnp.tanh(ROOT * (v + CUBIC * v * v * v))
    value = 0.5 * v * (1.0 + inner)
    slope = 0.5 * (1.0 + inner) + 0.5 * v * (1.0 - inner * inner) * ROOT * (
        1.0 + 3.0 * CUBIC * v * v
    )
    return value, slope


def up8(v):
    return lax.rem(v + 16, 8)


def drain(sent, stores):
    for cp in sent:
        cp.wait_send()
    for cp in stores:
        cp.wait()


def write_out(a, b, c, d, oa, ob, oc, od, sem):
    copies = [
        pltpu.make_async_copy(src, dst, sem.at[n])
        for n, (src, dst) in enumerate(((a, oa), (b, ob), (c, oc), (d, od)))
    ]
    for cp in copies:
        cp.start()
    for cp in copies:
        cp.wait()


def kernel(
    x_hbm, g_hbm, ut_hbm, dt_hbm, us_hbm, ds_hbm,
    mixed_out, gt_out, gu, gd,
    x_in, g_in, us, ds, ut, dt, w1, w2, xcar, gcar, xflat, gflat, xs, gs, xt, gt,
    part, rcore, sb, rx, hb, db, slopes, backs, htile, dtile,
    mcar, tcar, msend, mrecv, tsend, trecv, ms2, mr2, ts2, tr2, rows4,
    ssem, rsem, lsem,
):
    hid, wid = lax.axis_index("hid"), lax.axis_index("wid")
    z, y = lax.div(hid, 8), lax.rem(hid, 8)
    xx, c = lax.div(wid, 2), lax.rem(wid, 2)

    def at(zz, yy):
        return (up8(zz) * 8 + up8(yy), wid)

    def pair(pos, k):
        q = lax.div(pos, 2)
        return (q, q + 1 - 2 * lax.rem(q, 2), lax.rem(q + 2, 4), 3 - q)[k]

    def mate(pos, k, b):
        low = lax.rem(pos, 2)
        return pair(pos, k) * 2 + (1 - low if b else low)

    others = [(k, b) for k in FAR for b in (0, 1) if (k, b) != (0, 0)]
    xpeer = [(hid, lax.rem(xx + o, 4) * 2 + c) for o in (1, 2, 3)]
    xcross = [(hid, lax.rem(xx + o, 4) * 2 + 1 - c) for o in (1, 2, 3)]
    partner = (hid, xx * 2 + 1 - c)

    counter = [0]
    sent = []
    stores = []

    def rcopy(src, dst, dev):
        k = counter[0]
        counter[0] += 1
        cp = pltpu.make_async_remote_copy(
            src_ref=src, dst_ref=dst, send_sem=ssem.at[k], recv_sem=rsem.at[k],
            device_id=dev, device_id_type=MESH,
        )
        cp.start()
        sent.append(cp)
        return cp

    barrier = pltpu.get_barrier_semaphore()
    peers = [at(z, mate(y, k, b)) for k, b in others] + [at(mate(z, k, b), y) for k, b in others]
    peers += xpeer + xcross + [partner]
    for dev in peers:
        pl.semaphore_signal(barrier, inc=1, device_id=dev, device_id_type=MESH)

    loads = [
        pltpu.make_async_copy(a, b, lsem.at[n])
        for n, (a, b) in enumerate(
            (
                (x_hbm, x_in), (g_hbm, g_in), (us_hbm, us), (ds_hbm, ds),
                (ut_hbm.at[0, 0], ut), (dt_hbm.at[0, 0], dt),
            )
        )
    ]
    for cp in loads:
        cp.start()

    def to_rows(src, dst):
        val = src[...].astype(F32)
        for r in range(12):
            rows4[4 * r : 4 * r + 4, :] = val[:, r * 128 : (r + 1) * 128]
        dst[...] = rows4[...].astype(BF)

    loads[0].wait()
    to_rows(x_in, xcar.at[z, y])
    loads[1].wait()
    to_rows(g_in, gcar.at[y, z])
    pl.semaphore_wait(barrier, len(peers))

    first = {}
    for k, b in others:
        first["x", k, b] = rcopy(xcar.at[z, y], xcar.at[z, y], at(z, mate(y, k, b)))
        first["g", k, b] = rcopy(gcar.at[y, z], gcar.at[y, z], at(mate(z, k, b), y))

    for cp in loads[2:]:
        cp.wait()

    def build(slots, tiles, dense, rows, cols):
        def one(row, carry):
            pos = jnp.int32(0)
            for n in range(18):
                pos = pos + (slots[0, 0, n] < row * cols).astype(jnp.int32)
            for col in range(cols):
                idx = jnp.minimum(pos, 17)
                hit = jnp.logical_and(pos < 18, slots[0, 0, idx] == row * cols + col)
                tile = tiles[idx]
                dense[
                    pl.ds(pl.multiple_of(row * 128, 128), 128), col * 128 : (col + 1) * 128
                ] = jnp.where(hit, tile, jnp.zeros_like(tile))
                pos = pos + hit.astype(jnp.int32)
            return carry

        lax.fori_loop(0, rows, one, jnp.int32(0))

    build(us, ut, w1, 12, 6)
    build(ds, dt, w2, 6, 12)

    axes = {
        "x": (xcar, z, y, lambda d: at(z + d, y)),
        "g": (gcar, y, z, lambda d: at(z, y + d)),
    }
    ring = {}

    def offsets(g):
        return (-g, g + 1)

    def settle(keep=0):
        for cp in sent[: len(sent) - keep]:
            cp.wait_send()
        del sent[: len(sent) - keep]

    def run(tasks, share):
        for _ in range(min(len(tasks), share)):
            tasks.pop(0)()

    def step(s, tasks=()):
        tasks = list(tasks)
        share = -(-len(tasks) // 5)
        run(tasks, share)
        for k in NEAR:
            for name in ("x", "g"):
                car, pos, cross, dev = axes[name]
                span = pl.ds(pair(cross, k) * 2, 2)

                def forward(slab, hops, key):
                    ref = car.at[up8(slab), span]
                    ring[(name, k) + key] = rcopy(ref, ref, dev(hops))

                if s == 0:
                    for b in (0, 1):
                        if (k, b) != (0, 0):
                            first[name, k, b].wait_recv()
                else:
                    for way in (0, 1):
                        if s <= REACH[k][way]:
                            ring[name, k, s - 1, way].wait_recv()
                    if s == 4 and k in SKIP:
                        ring[name, k, 2, 2].wait_recv()
                if s == 2 and k in SKIP:
                    way = 1 if k == 2 else -1
                    forward(pos - 2 * way, 2 * way, (2, 2))
                for way in (0, 1):
                    if s < REACH[k][way]:
                        sign = 1 - 2 * way
                        forward(pos - sign * s, sign, (s, way))
            run(tasks, share)

    def widen(car, pos, flat, off):
        d = up8(pos + off)
        flat[pl.ds(pl.multiple_of(d * 384, 384), 384), :] = car[d].reshape(384, 128).astype(F32)

    def unpack(pos, flat, dst, g, tiles):
        for r in tiles:
            for i in range(4):
                rows = [
                    flat[pl.ds(up8(pos + off) * 384 + 4 * r + i, 8, stride=48), :]
                    for off in offsets(g)
                ]
                dst[g, i * 16 : (i + 1) * 16, r * 128 : (r + 1) * 128] = jnp.concatenate(
                    rows, axis=0
                ).astype(BF)

    core = {}
    over = {}
    back_home = {}

    def product(a, g, q):
        cols = slice(q * 256, (q + 1) * 256)
        if a == 0:
            val = jnp.dot(xs[g], w1[:, cols], preferred_element_type=F32)
        else:
            val = lax.dot_general(
                gs[g], w2[cols, :], (((1,), (1,)), ((), ())), preferred_element_type=F32
            )
        for t in range(2):
            n = 2 * q + t
            part[g, n // 3, a, :, (n % 3) * 128 : (n % 3 + 1) * 128] = val[
                :, t * 128 : (t + 1) * 128
            ]
        if q == 2:
            core[g, a] = rcopy(part.at[g, 1 - c, a], rcore.at[g, a], partner)

    def compute(g, a):
        car, pos, flat, dst = ((xcar, z, xflat, xs), (gcar, y, gflat, gs))[a]
        tasks = [functools.partial(widen, car, pos, flat, off) for off in offsets(g)]
        for t in range(4):
            tasks.append(
                functools.partial(unpack, pos, flat, dst, g, (3 * t, 3 * t + 1, 3 * t + 2))
            )
        return tasks + [functools.partial(product, a, g, q) for q in range(3)]

    def compute_now(g, a):
        for task in compute(g, a):
            task()

    def sum_cores(g, a):
        core[g, a].wait_recv()
        total = part[g, c, a] + rcore[g, a]
        rcore[g, a] = total
        for i in range(4):
            sb[g, i, a] = total[i * 16 : (i + 1) * 16].astype(BF)
        for dev, o in zip(xpeer, (1, 2, 3)):
            over[g, a, o] = rcopy(sb.at[g, lax.rem(xx + o, 4), a], rx.at[g, o, a], dev)

    def mine(buf, g, i):
        return buf.at[
            g,
            pl.ds(pl.multiple_of(i * 16, 16), 16),
            pl.ds(pl.multiple_of(c * 384, 128), 384),
        ]

    def send_home(buf, name, g):
        ref = mine(buf, g, xx)
        devs = xpeer + [partner] + (xcross if g == 3 else [])
        back_home[name, g] = [rcopy(ref, ref, dev) for dev in devs]

    def relay(buf, name, g):
        for n, o in enumerate((1, 2, 3)):
            back_home[name, g][n].wait_recv()
            ref = mine(buf, g, lax.rem(xx + 4 - o, 4))
            back_home[name, g].append(rcopy(ref, ref, partner))

    def all_home(name, g):
        for cp in back_home[name, g][0 if g == 3 else 3 :]:
            cp.wait_recv()

    def sum_chips(g, a):
        acc = rcore[g, a, pl.ds(pl.multiple_of(xx * 16, 16), 16), :]
        for o in (1, 2, 3):
            over[g, a, o].wait_recv()
            acc = acc + rx[g, o, a].astype(F32)
        return acc

    def lay(buf, val, pos, g):
        for n, off in enumerate(offsets(g)):
            d = up8(pos + off)
            for t in range(3):
                buf[t, pl.ds(pl.multiple_of(d * 8, 8), 8), :] = val[
                    n * 8 : (n + 1) * 8, t * 128 : (t + 1) * 128
                ]

    def hidden(g):
        value, slope = gelu_both(sum_chips(g, 0))
        ref = mine(hb, g, xx)
        ref[...] = value.astype(BF)
        send_home(hb, "h", g)
        lay(slopes, slope, z, g)

    def delta(g):
        lay(backs, sum_chips(g, 1), y, g)
        rows = []
        for off in offsets(g):
            dy = up8(y + off)
            rows.append(
                jnp.concatenate(
                    [
                        backs[t, pl.ds(pl.multiple_of(dy * 8, 8), 8), :]
                        * slopes[t, pl.ds(dy, 8, stride=8), :]
                        for t in range(3)
                    ],
                    axis=1,
                )
            )
        ref = mine(db, g, xx)
        ref[...] = jnp.concatenate(rows, axis=0).astype(BF)
        send_home(db, "d", g)

    def retile(flat, pos, dst):
        def one(g, carry):
            for r in range(12):
                for i in range(4):
                    rows = [
                        flat[pl.ds(up8(pos - g + n * (2 * g + 1)) * 48 + 4 * r + i, 8, stride=384), :]
                        for n in range(2)
                    ]
                    dst[r, pl.ds(pl.multiple_of(g * 64 + i * 16, 16), 16), :] = jnp.concatenate(
                        rows, axis=0
                    ).astype(BF)
            return carry

        lax.fori_loop(0, 4, one, jnp.int32(0))

    def pack(val, r, car, pos, groups):
        for n, g in enumerate(groups):
            for i in range(4):
                for m, off in enumerate(offsets(g)):
                    lo = n * 64 + i * 16 + m * 8
                    car[pl.ds(up8(pos + off) * 384 + 4 * r + i, 8, stride=48), :] = val[lo : lo + 8]

    def mixed_part(groups):
        lhs = jnp.concatenate([hb[g] for g in groups], axis=0)

        def cols(q, carry):
            val = jnp.dot(
                lhs, w2[:, pl.ds(pl.multiple_of(q * 256, 256), 256)], preferred_element_type=F32
            )
            pack(val[:, :128], 2 * q, mcar, z, groups)
            pack(val[:, 128:], 2 * q + 1, mcar, z, groups)
            return carry

        for q in range(6):
            cols(q, 0)

    def back_part(groups):
        lhs = jnp.concatenate([db[g] for g in groups], axis=0)

        def cols(q, carry):
            val = lax.dot_general(
                lhs,
                w1[pl.ds(pl.multiple_of(q * 256, 256), 256), :],
                (((1,), (1,)), ((), ())),
                preferred_element_type=F32,
            )
            pack(val[:, :128], 2 * q, tcar, y, groups)
            pack(val[:, 128:], 2 * q + 1, tcar, y, groups)
            return carry

        for q in range(6):
            cols(q, 0)

    outs = {
        "m": (mcar, msend, mrecv, z, y, lambda d: at(z + d, y), ms2, mr2),
        "t": (tcar, tsend, trecv, y, z, lambda d: at(z, y + d), ts2, tr2),
    }
    rsum = {}
    last = {}

    def block(name, k, d):
        car, pos, cross = outs[name][0], outs[name][3], outs[name][4]
        return pl.ds(pl.multiple_of(up8(pos + d) * 384 + pair(cross, k) * 96, 96), 96)

    def span_of(name, k):
        return pl.ds(pl.multiple_of(pair(outs[name][4], k) * 96, 96), 96)

    def got(name, k, way, s):
        rsum[name, k, way, s].wait_recv()
        return outs[name][2][way, s, span_of(name, k), :].astype(F32)

    def ring_send(name, k, s):
        car, send, recv, pos, cross, dev, _, _ = outs[name]
        span = span_of(name, k)

        def push(val, way, hops):
            send[way, s, span, :] = val.astype(BF)
            rsum[name, k, way, s] = rcopy(
                send.at[way, s, span, :], recv.at[way, s, span, :], dev(hops)
            )

        far_way = SHORT.index(k) if k in SHORT else None
        if s == 0 and k in SHORT:
            push(car[block(name, k, 4), :], 2, 2 - 4 * far_way)
        for way in (0, 1):
            reach = SUMS[k][way] - s
            if reach < 1:
                continue
            val = car[block(name, k, reach if way == 0 else -reach), :]
            if s > 0:
                val = val + got(name, k, way, s - 1)
            if s == 1 and far_way == way:
                val = val + got(name, k, 2, 0)
            push(val, way, 1 - 2 * way)

    def ring_end(name, k):
        car, _, _, pos, cross, _, send2, recv2 = outs[name]
        span = span_of(name, k)
        here = block(name, k, 0)
        val = car[here, :] + got(name, k, 0, SUMS[k][0] - 1) + got(name, k, 1, SUMS[k][1] - 1)
        car[here, :] = val
        send2[span, :] = val.astype(BF)
        for b in (0, 1):
            if (k, b) == (0, 0):
                continue
            to = mate(cross, k, b)
            dev = at(pos, to) if name == "m" else at(to, pos)
            last[name, k, b] = rcopy(
                send2.at[pl.ds(pl.multiple_of(to * 48, 48), 48), :], recv2.at[2 * k + b], dev
            )

    def ring_step(s, names=("m", "t"), pairs=ORDER, tasks=()):
        tasks = list(tasks)
        share = -(-len(tasks) // len(pairs))
        for k in pairs:
            for name in names:
                if s == 3 and k in SHORT:
                    ring_end(name, k)
                elif s == 4:
                    ring_end(name, k)
                else:
                    ring_send(name, k, s)
            run(tasks, share)

    def up_some(lo, hi):
        def one(n):
            slot = us[0, 0, n]
            lhs, rhs = xt[lax.div(slot, 6)], dtile[lax.rem(slot, 6)]
            gu[0, 0, n] = lax.dot_general(
                lhs, rhs, (((0,), (0,)), ((), ())), preferred_element_type=F32
            )

        def six(t, carry):
            for n in range(6):
                one(lo + 6 * t + n)
            return carry

        lax.fori_loop(0, (hi - lo) // 6, six, jnp.int32(0))

    def down_some(lo, hi):
        def one(n):
            slot = ds[0, 0, n]
            lhs, rhs = htile[lax.div(slot, 12)], gt[lax.rem(slot, 12)]
            gd[0, 0, n] = lax.dot_general(
                lhs, rhs, (((0,), (0,)), ((), ())), preferred_element_type=F32
            )

        def six(t, carry):
            for n in range(6):
                one(lo + 6 * t + n)
            return carry

        lax.fori_loop(0, (hi - lo) // 6, six, jnp.int32(0))

    def tile_up(buf, dst):
        for b in range(6):
            dst[b] = buf[:, :, b * 128 : (b + 1) * 128].reshape(256, 128)

    P_ = functools.partial
    step(0)
    step(1)
    step(2, compute(0, 0))
    todo = compute(1, 0)
    step(3, todo[:5] + [P_(sum_cores, 0, 0)] + todo[5:])
    todo = compute(2, 0)
    step(4, todo[:5] + [P_(sum_cores, 1, 0)] + todo[5:])
    compute_now(3, 0)
    sum_cores(2, 0)
    compute_now(3, 1)
    sum_cores(3, 0)
    compute_now(2, 1)
    sum_cores(3, 1)
    hidden(0)
    compute_now(1, 1)
    sum_cores(2, 1)
    hidden(1)
    compute_now(0, 1)
    sum_cores(1, 1)
    hidden(2)
    sum_cores(0, 1)
    relay(hb, "h", 0)
    hidden(3)
    delta(3)
    relay(hb, "h", 1)
    delta(2)
    retile(xflat, y, xt)
    delta(1)
    delta(0)
    for g in (1, 0):
        all_home("h", g)
    mixed_part((1, 0))
    settle(60)
    relay(hb, "h", 2)
    all_home("h", 3)
    mixed_part((3,))
    ring_step(0, names=("m",))
    all_home("d", 3)
    back_part((3,))
    ring_step(0, names=("t",))
    relay(db, "d", 2)
    all_home("h", 2)
    mixed_part((2,))
    all_home("d", 2)
    back_part((2,))
    ring_step(1)
    relay(db, "d", 1)
    relay(db, "d", 0)
    for g in (1, 0):
        all_home("d", g)
    back_part((1, 0))
    ring_step(2)
    settle(40)
    tile_up(db, dtile)
    up_some(0, 6)
    ring_step(3)
    up_some(6, 18)
    ring_step(4)
    tile_up(hb, htile)
    retile(gflat, z, gt)
    down_some(0, 18)
    settle(14)

    def finish(name, recv2, out):
        car, _, _, pos, cross, _, _, _ = outs[name]
        acc = car[pl.ds(pl.multiple_of(pos * 384 + cross * 48, 48), 48), :]
        for k, b in others:
            last[name, k, b].wait_recv()
            acc = acc + recv2[2 * k + b].astype(F32)
        rows4[...] = acc
        cols = [rows4[4 * r : 4 * r + 4, :] for r in range(12)]
        out[...] = jnp.concatenate(cols, axis=1).astype(BF)

    finish("m", mr2, mixed_out)
    finish("t", tr2, gt_out)
    drain(sent, stores)


N_COPIES = 14 + 56 + 8 + 24 + 56 + 56 + 14 + 16


def per_device(tokens, out_grad, up_tiles, down_tiles, up_slots, down_slots):
    vmem = pl.BlockSpec(memory_space=pltpu.VMEM)
    hbm = pl.BlockSpec(memory_space=pltpu.HBM)
    V = pltpu.VMEM
    results = pl.pallas_call(
        kernel,
        out_shape=(
            V((4, 1536), BF),
            V((4, 1536), BF),
            V((1, 1, 18, 128, 128), F32),
            V((1, 1, 18, 128, 128), F32),
        ),
        in_specs=[hbm] * 6,
        out_specs=(vmem,) * 4,
        scratch_shapes=[
            V((4, 1536), BF),
            V((4, 1536), BF),
            pltpu.SMEM((1, 1, 18), jnp.int32),
            pltpu.SMEM((1, 1, 18), jnp.int32),
            V((18, 128, 128), BF),
            V((18, 128, 128), BF),
            V((1536, 768), BF),
            V((768, 1536), BF),
            V((8, 8, 48, 128), BF),
            V((8, 8, 48, 128), BF),
            V((3072, 128), F32),
            V((3072, 128), F32),
            V((4, 64, 1536), BF),
            V((4, 64, 1536), BF),
            V((12, 256, 128), BF),
            V((12, 256, 128), BF),
            V((4, 2, 2, 64, 384), F32),
            V((4, 2, 64, 384), F32),
            V((4, 4, 2, 16, 384), BF),
            V((4, 4, 2, 16, 384), BF),
            V((4, 64, 768), BF),
            V((4, 64, 768), BF),
            V((3, 64, 128), F32),
            V((3, 64, 128), F32),
            V((6, 256, 128), BF),
            V((6, 256, 128), BF),
            V((3072, 128), F32),
            V((3072, 128), F32),
            V((3, 4, 384, 128), BF),
            V((3, 4, 384, 128), BF),
            V((3, 4, 384, 128), BF),
            V((3, 4, 384, 128), BF),
            V((384, 128), BF),
            V((8, 48, 128), BF),
            V((384, 128), BF),
            V((8, 48, 128), BF),
            V((48, 128), F32),
            pltpu.SemaphoreType.DMA((N_COPIES,)),
            pltpu.SemaphoreType.DMA((N_COPIES,)),
            pltpu.SemaphoreType.DMA((8,)),
        ],
        compiler_params=pltpu.CompilerParams(
            collective_id=0, has_side_effects=True, vmem_limit_bytes=40 * 1024 * 1024
        ),
    )(
        *(
            pltpu.with_memory_space_constraint(a, pltpu.HBM)
            for a in (tokens, out_grad, up_tiles, down_tiles, up_slots, down_slots)
        )
    )
    return pl.pallas_call(
        write_out,
        out_shape=tuple(jax.ShapeDtypeStruct(r.shape, r.dtype) for r in results),
        in_specs=[vmem] * 4,
        out_specs=(hbm,) * 4,
        scratch_shapes=[pltpu.SemaphoreType.DMA((4,))],
        compiler_params=pltpu.CompilerParams(vmem_limit_bytes=4 * 1024 * 1024),
    )(*(pltpu.with_memory_space_constraint(r, pltpu.VMEM) for r in results))


def solution(mesh):
    spec2, spec5, spec3 = P("hid", "wid"), P("hid", "wid", None, None, None), P("hid", "wid", None)
    return jax.shard_map(
        per_device,
        mesh=mesh,
        in_specs=(spec2, spec2, spec5, spec5, spec3, spec3),
        out_specs=(spec2, spec2, spec5, spec5),
        check_vma=False,
    )
```

```python
import functools

import jax
import jax.numpy as jnp
from jax import lax
from jax.experimental import pallas as pl
from jax.experimental.pallas import tpu as pltpu
from jax.sharding import PartitionSpec as P

MESH = pl.DeviceIdType.MESH
BF = jnp.bfloat16
F32 = jnp.float32

ROOT = 0.7978845608028654
CUBIC = 0.044715

NEAR = (0, 1, 3, 2)
FAR = (2, 3, 1, 0)
ORDER = FAR
SKIP = (1, 2, 3)
REACH = ((4, 3), (3, 3), (3, 3), (3, 3))
SHORT = ()
SUMS = ((4, 3),) * 4


def gelu_both(v):
    inner = jnp.tanh(ROOT * (v + CUBIC * v * v * v))
    value = 0.5 * v * (1.0 + inner)
    slope = 0.5 * (1.0 + inner) + 0.5 * v * (1.0 - inner * inner) * ROOT * (
        1.0 + 3.0 * CUBIC * v * v
    )
    return value, slope


def up8(v):
    return lax.rem(v + 16, 8)


def drain(sent, stores):
    for cp in sent:
        cp.wait_send()
    for cp in stores:
        cp.wait()


def write_out(a, b, c, d, oa, ob, oc, od, sem):
    copies = [
        pltpu.make_async_copy(src, dst, sem.at[n])
        for n, (src, dst) in enumerate(((a, oa), (b, ob), (c, oc), (d, od)))
    ]
    for cp in copies:
        cp.start()
    for cp in copies:
        cp.wait()


def kernel(
    x_hbm, g_hbm, ut_hbm, dt_hbm, us_hbm, ds_hbm,
    mixed_out, gt_out, gu, gd,
    x_in, g_in, us, ds, ut, dt, w1, w2, xcar, gcar, xflat, gflat, xs, gs, xt, gt,
    part, rcore, sb, rx, hb, db, slopes, backs, htile, dtile,
    mcar, tcar, msend, mrecv, tsend, trecv, ms2, mr2, ts2, tr2, rows4,
    ssem, rsem, lsem,
):
    hid, wid = lax.axis_index("hid"), lax.axis_index("wid")
    z, y = lax.div(hid, 8), lax.rem(hid, 8)
    xx, c = lax.div(wid, 2), lax.rem(wid, 2)

    def at(zz, yy):
        return (up8(zz) * 8 + up8(yy), wid)

    def pair(pos, k):
        q = lax.div(pos, 2)
        return (q, q + 1 - 2 * lax.rem(q, 2), lax.rem(q + 2, 4), 3 - q)[k]

    def mate(pos, k, b):
        low = lax.rem(pos, 2)
        return pair(pos, k) * 2 + (1 - low if b else low)

    others = [(k, b) for k in NEAR for b in (0, 1) if (k, b) != (0, 0)]
    xpeer = [(hid, lax.rem(xx + o, 4) * 2 + c) for o in (1, 2, 3)]
    xcross = [(hid, lax.rem(xx + o, 4) * 2 + 1 - c) for o in (1, 2, 3)]
    partner = (hid, xx * 2 + 1 - c)

    counter = [0]
    sent = []
    stores = []

    def rcopy(src, dst, dev):
        k = counter[0]
        counter[0] += 1
        cp = pltpu.make_async_remote_copy(
            src_ref=src, dst_ref=dst, send_sem=ssem.at[k], recv_sem=rsem.at[k],
            device_id=dev, device_id_type=MESH,
        )
        cp.start()
        sent.append(cp)
        return cp

    barrier = pltpu.get_barrier_semaphore()
    peers = [at(z, mate(y, k, b)) for k, b in others] + [at(mate(z, k, b), y) for k, b in others]
    peers += xpeer + xcross + [partner]
    for dev in peers:
        pl.semaphore_signal(barrier, inc=1, device_id=dev, device_id_type=MESH)

    loads = [
        pltpu.make_async_copy(a, b, lsem.at[n])
        for n, (a, b) in enumerate(
            (
                (x_hbm, x_in), (g_hbm, g_in), (us_hbm, us), (ds_hbm, ds),
                (ut_hbm.at[0, 0], ut), (dt_hbm.at[0, 0], dt),
            )
        )
    ]
    for cp in loads:
        cp.start()

    def to_rows(src, dst):
        val = src[...].astype(F32)
        for r in range(12):
            rows4[4 * r : 4 * r + 4, :] = val[:, r * 128 : (r + 1) * 128]
        dst[...] = rows4[...].astype(BF)

    loads[0].wait()
    to_rows(x_in, xcar.at[z, y])
    loads[1].wait()
    to_rows(g_in, gcar.at[y, z])
    pl.semaphore_wait(barrier, len(peers))

    first = {}
    for k, b in others:
        first["x", k, b] = rcopy(xcar.at[z, y], xcar.at[z, y], at(z, mate(y, k, b)))
        first["g", k, b] = rcopy(gcar.at[y, z], gcar.at[y, z], at(mate(z, k, b), y))

    for cp in loads[2:]:
        cp.wait()

    def build(slots, tiles, dense, rows, cols):
        def one(row, carry):
            pos = jnp.int32(0)
            for n in range(18):
                pos = pos + (slots[0, 0, n] < row * cols).astype(jnp.int32)
            for col in range(cols):
                idx = jnp.minimum(pos, 17)
                hit = jnp.logical_and(pos < 18, slots[0, 0, idx] == row * cols + col)
                tile = tiles[idx]
                dense[
                    pl.ds(pl.multiple_of(row * 128, 128), 128), col * 128 : (col + 1) * 128
                ] = jnp.where(hit, tile, jnp.zeros_like(tile))
                pos = pos + hit.astype(jnp.int32)
            return carry

        lax.fori_loop(0, rows, one, jnp.int32(0))

    build(us, ut, w1, 12, 6)
    build(ds, dt, w2, 6, 12)

    axes = {
        "x": (xcar, z, y, lambda d: at(z + d, y)),
        "g": (gcar, y, z, lambda d: at(z, y + d)),
    }
    ring = {}

    def offsets(g):
        return (-g, g + 1)

    def settle(keep=0):
        for cp in sent[: len(sent) - keep]:
            cp.wait_send()
        del sent[: len(sent) - keep]

    def run(tasks, share):
        for _ in range(min(len(tasks), share)):
            tasks.pop(0)()

    def step(s, tasks=()):
        tasks = list(tasks)
        share = -(-len(tasks) // 5)
        run(tasks, share)
        for k in NEAR:
            for name in ("x", "g"):
                car, pos, cross, dev = axes[name]
                span = pl.ds(pair(cross, k) * 2, 2)

                def forward(slab, hops, key):
                    ref = car.at[up8(slab), span]
                    ring[(name, k) + key] = rcopy(ref, ref, dev(hops))

                if s == 0:
                    for b in (0, 1):
                        if (k, b) != (0, 0):
                            first[name, k, b].wait_recv()
                else:
                    for way in (0, 1):
                        if s <= REACH[k][way]:
                            ring[name, k, s - 1, way].wait_recv()
                    if s == 4 and k in SKIP:
                        ring[name, k, 2, 2].wait_recv()
                if s == 2 and k in SKIP:
                    way = -1 if k == 3 else 1
                    forward(pos - 2 * way, 2 * way, (2, 2))
                for way in (0, 1):
                    if s < REACH[k][way]:
                        sign = 1 - 2 * way
                        forward(pos - sign * s, sign, (s, way))
            run(tasks, share)

    def widen(car, pos, flat, off):
        d = up8(pos + off)
        flat[pl.ds(pl.multiple_of(d * 384, 384), 384), :] = car[d].reshape(384, 128).astype(F32)

    def unpack(pos, flat, dst, g, tiles):
        for r in tiles:
            for i in range(4):
                rows = [
                    flat[pl.ds(up8(pos + off) * 384 + 4 * r + i, 8, stride=48), :]
                    for off in offsets(g)
                ]
                dst[g, i * 16 : (i + 1) * 16, r * 128 : (r + 1) * 128] = jnp.concatenate(
                    rows, axis=0
                ).astype(BF)

    core = {}
    over = {}
    back_home = {}

    def product(a, g, q):
        cols = slice(q * 256, (q + 1) * 256)
        if a == 0:
            val = jnp.dot(xs[g], w1[:, cols], preferred_element_type=F32)
        else:
            val = lax.dot_general(
                gs[g], w2[cols, :], (((1,), (1,)), ((), ())), preferred_element_type=F32
            )
        for t in range(2):
            n = 2 * q + t
            part[g, n // 3, a, :, (n % 3) * 128 : (n % 3 + 1) * 128] = val[
                :, t * 128 : (t + 1) * 128
            ]
        if q == 2:
            core[g, a] = rcopy(part.at[g, 1 - c, a], rcore.at[g, a], partner)

    def compute(g, a):
        car, pos, flat, dst = ((xcar, z, xflat, xs), (gcar, y, gflat, gs))[a]
        tasks = [functools.partial(widen, car, pos, flat, off) for off in offsets(g)]
        for t in range(4):
            tasks.append(
                functools.partial(unpack, pos, flat, dst, g, (3 * t, 3 * t + 1, 3 * t + 2))
            )
        return tasks + [functools.partial(product, a, g, q) for q in range(3)]

    def compute_now(g, a):
        for task in compute(g, a):
            task()

    def sum_cores(g, a):
        core[g, a].wait_recv()
        total = part[g, c, a] + rcore[g, a]
        rcore[g, a] = total
        for i in range(4):
            sb[g, i, a] = total[i * 16 : (i + 1) * 16].astype(BF)
        for dev, o in zip(xpeer, (1, 2, 3)):
            over[g, a, o] = rcopy(sb.at[g, lax.rem(xx + o, 4), a], rx.at[g, o, a], dev)

    def mine(buf, g, i):
        return buf.at[
            g,
            pl.ds(pl.multiple_of(i * 16, 16), 16),
            pl.ds(pl.multiple_of(c * 384, 128), 384),
        ]

    def send_home(buf, name, g):
        ref = mine(buf, g, xx)
        devs = xpeer + [partner] + (xcross if g == 3 else [])
        back_home[name, g] = [rcopy(ref, ref, dev) for dev in devs]

    def relay(buf, name, g):
        for n, o in enumerate((1, 2, 3)):
            back_home[name, g][n].wait_recv()
            ref = mine(buf, g, lax.rem(xx + 4 - o, 4))
            back_home[name, g].append(rcopy(ref, ref, partner))

    def all_home(name, g):
        for cp in back_home[name, g][0 if g == 3 else 3 :]:
            cp.wait_recv()

    def sum_chips(g, a):
        acc = rcore[g, a, pl.ds(pl.multiple_of(xx * 16, 16), 16), :]
        for o in (1, 2, 3):
            over[g, a, o].wait_recv()
            acc = acc + rx[g, o, a].astype(F32)
        return acc

    def lay(buf, val, pos, g):
        for n, off in enumerate(offsets(g)):
            d = up8(pos + off)
            for t in range(3):
                buf[t, pl.ds(pl.multiple_of(d * 8, 8), 8), :] = val[
                    n * 8 : (n + 1) * 8, t * 128 : (t + 1) * 128
                ]

    def hidden(g):
        value, slope = gelu_both(sum_chips(g, 0))
        ref = mine(hb, g, xx)
        ref[...] = value.astype(BF)
        send_home(hb, "h", g)
        lay(slopes, slope, z, g)

    def delta(g):
        lay(backs, sum_chips(g, 1), y, g)
        rows = []
        for off in offsets(g):
            dy = up8(y + off)
            rows.append(
                jnp.concatenate(
                    [
                        backs[t, pl.ds(pl.multiple_of(dy * 8, 8), 8), :]
                        * slopes[t, pl.ds(dy, 8, stride=8), :]
                        for t in range(3)
                    ],
                    axis=1,
                )
            )
        ref = mine(db, g, xx)
        ref[...] = jnp.concatenate(rows, axis=0).astype(BF)
        send_home(db, "d", g)

    def retile(flat, pos, dst):
        def one(g, carry):
            for r in range(12):
                for i in range(4):
                    rows = [
                        flat[pl.ds(up8(pos - g + n * (2 * g + 1)) * 48 + 4 * r + i, 8, stride=384), :]
                        for n in range(2)
                    ]
                    dst[r, pl.ds(pl.multiple_of(g * 64 + i * 16, 16), 16), :] = jnp.concatenate(
                        rows, axis=0
                    ).astype(BF)
            return carry

        lax.fori_loop(0, 4, one, jnp.int32(0))

    def pack(val, r, car, pos, groups):
        for n, g in enumerate(groups):
            for i in range(4):
                for m, off in enumerate(offsets(g)):
                    lo = n * 64 + i * 16 + m * 8
                    car[pl.ds(up8(pos + off) * 384 + 4 * r + i, 8, stride=48), :] = val[lo : lo + 8]

    def mixed_part(groups):
        lhs = jnp.concatenate([hb[g] for g in groups], axis=0)

        def cols(q, carry):
            val = jnp.dot(
                lhs, w2[:, pl.ds(pl.multiple_of(q * 256, 256), 256)], preferred_element_type=F32
            )
            pack(val[:, :128], 2 * q, mcar, z, groups)
            pack(val[:, 128:], 2 * q + 1, mcar, z, groups)
            return carry

        for q in range(6):
            cols(q, 0)

    def back_part(groups):
        lhs = jnp.concatenate([db[g] for g in groups], axis=0)

        def cols(q, carry):
            val = lax.dot_general(
                lhs,
                w1[pl.ds(pl.multiple_of(q * 256, 256), 256), :],
                (((1,), (1,)), ((), ())),
                preferred_element_type=F32,
            )
            pack(val[:, :128], 2 * q, tcar, y, groups)
            pack(val[:, 128:], 2 * q + 1, tcar, y, groups)
            return carry

        for q in range(6):
            cols(q, 0)

    outs = {
        "m": (mcar, msend, mrecv, z, y, lambda d: at(z + d, y), ms2, mr2),
        "t": (tcar, tsend, trecv, y, z, lambda d: at(z, y + d), ts2, tr2),
    }
    rsum = {}
    last = {}

    def block(name, k, d):
        car, pos, cross = outs[name][0], outs[name][3], outs[name][4]
        return pl.ds(pl.multiple_of(up8(pos + d) * 384 + pair(cross, k) * 96, 96), 96)

    def span_of(name, k):
        return pl.ds(pl.multiple_of(pair(outs[name][4], k) * 96, 96), 96)

    def got(name, k, way, s):
        rsum[name, k, way, s].wait_recv()
        return outs[name][2][way, s, span_of(name, k), :].astype(F32)

    def ring_send(name, k, s):
        car, send, recv, pos, cross, dev, _, _ = outs[name]
        span = span_of(name, k)

        def push(val, way, hops):
            send[way, s, span, :] = val.astype(BF)
            rsum[name, k, way, s] = rcopy(
                send.at[way, s, span, :], recv.at[way, s, span, :], dev(hops)
            )

        far_way = SHORT.index(k) if k in SHORT else None
        if s == 0 and k in SHORT:
            push(car[block(name, k, 4), :], 2, 2 - 4 * far_way)
        for way in (0, 1):
            reach = SUMS[k][way] - s
            if reach < 1:
                continue
            val = car[block(name, k, reach if way == 0 else -reach), :]
            if s > 0:
                val = val + got(name, k, way, s - 1)
            if s == 1 and far_way == way:
                val = val + got(name, k, 2, 0)
            push(val, way, 1 - 2 * way)

    def ring_end(name, k):
        car, _, _, pos, cross, _, send2, recv2 = outs[name]
        span = span_of(name, k)
        here = block(name, k, 0)
        val = car[here, :] + got(name, k, 0, SUMS[k][0] - 1) + got(name, k, 1, SUMS[k][1] - 1)
        car[here, :] = val
        send2[span, :] = val.astype(BF)
        for b in (0, 1):
            if (k, b) == (0, 0):
                continue
            to = mate(cross, k, b)
            dev = at(pos, to) if name == "m" else at(to, pos)
            last[name, k, b] = rcopy(
                send2.at[pl.ds(pl.multiple_of(to * 48, 48), 48), :], recv2.at[2 * k + b], dev
            )

    def ring_step(s, names=("m", "t"), pairs=ORDER, tasks=()):
        tasks = list(tasks)
        share = -(-len(tasks) // len(pairs))
        for k in pairs:
            for name in names:
                if s == 3 and k in SHORT:
                    ring_end(name, k)
                elif s == 4:
                    ring_end(name, k)
                else:
                    ring_send(name, k, s)
            run(tasks, share)

    def up_some(lo, hi):
        def one(n):
            slot = us[0, 0, n]
            lhs, rhs = xt[lax.div(slot, 6)], dtile[lax.rem(slot, 6)]
            gu[0, 0, n] = lax.dot_general(
                lhs, rhs, (((0,), (0,)), ((), ())), preferred_element_type=F32
            )

        def six(t, carry):
            for n in range(6):
                one(lo + 6 * t + n)
            return carry

        lax.fori_loop(0, (hi - lo) // 6, six, jnp.int32(0))

    def down_some(lo, hi):
        def one(n):
            slot = ds[0, 0, n]
            lhs, rhs = htile[lax.div(slot, 12)], gt[lax.rem(slot, 12)]
            gd[0, 0, n] = lax.dot_general(
                lhs, rhs, (((0,), (0,)), ((), ())), preferred_element_type=F32
            )

        def six(t, carry):
            for n in range(6):
                one(lo + 6 * t + n)
            return carry

        lax.fori_loop(0, (hi - lo) // 6, six, jnp.int32(0))

    def tile_up(buf, dst):
        for b in range(6):
            dst[b] = buf[:, :, b * 128 : (b + 1) * 128].reshape(256, 128)

    P_ = functools.partial
    step(0)
    step(1)
    step(2, compute(0, 0))
    todo = compute(1, 0)
    step(3, todo[:5] + [P_(sum_cores, 0, 0)] + todo[5:])
    todo = compute(2, 0)
    step(4, todo[:5] + [P_(sum_cores, 1, 0)] + todo[5:])
    compute_now(3, 0)
    sum_cores(2, 0)
    compute_now(3, 1)
    sum_cores(3, 0)
    compute_now(2, 1)
    sum_cores(3, 1)
    hidden(0)
    compute_now(1, 1)
    sum_cores(2, 1)
    hidden(1)
    compute_now(0, 1)
    sum_cores(1, 1)
    hidden(2)
    sum_cores(0, 1)
    relay(hb, "h", 0)
    hidden(3)
    delta(3)
    relay(hb, "h", 1)
    delta(2)
    delta(1)
    delta(0)
    for g in (1, 0):
        all_home("h", g)
    mixed_part((1, 0))
    settle(60)
    relay(hb, "h", 2)
    all_home("h", 3)
    mixed_part((3,))
    ring_step(0, names=("m",))
    all_home("d", 3)
    back_part((3,))
    ring_step(0, names=("t",))
    relay(db, "d", 2)
    all_home("h", 2)
    mixed_part((2,))
    all_home("d", 2)
    back_part((2,))
    ring_step(1)
    relay(db, "d", 1)
    relay(db, "d", 0)
    for g in (1, 0):
        all_home("d", g)
    back_part((1, 0))
    ring_step(2)
    settle(40)
    retile(xflat, y, xt)
    ring_step(3)
    tile_up(db, dtile)
    up_some(0, 12)
    ring_step(4)
    tile_up(hb, htile)
    retile(gflat, z, gt)
    up_some(12, 18)
    down_some(0, 18)
    settle(14)

    def finish(name, recv2, out):
        car, _, _, pos, cross, _, _, _ = outs[name]
        acc = car[pl.ds(pl.multiple_of(pos * 384 + cross * 48, 48), 48), :]
        for k, b in others:
            last[name, k, b].wait_recv()
            acc = acc + recv2[2 * k + b].astype(F32)
        rows4[...] = acc
        cols = [rows4[4 * r : 4 * r + 4, :] for r in range(12)]
        out[...] = jnp.concatenate(cols, axis=1).astype(BF)

    finish("m", mr2, mixed_out)
    finish("t", tr2, gt_out)
    drain(sent, stores)


N_COPIES = 14 + 56 + 8 + 24 + 56 + 56 + 14 + 16


def per_device(tokens, out_grad, up_tiles, down_tiles, up_slots, down_slots):
    vmem = pl.BlockSpec(memory_space=pltpu.VMEM)
    hbm = pl.BlockSpec(memory_space=pltpu.HBM)
    V = pltpu.VMEM
    results = pl.pallas_call(
        kernel,
        out_shape=(
            V((4, 1536), BF),
            V((4, 1536), BF),
            V((1, 1, 18, 128, 128), F32),
            V((1, 1, 18, 128, 128), F32),
        ),
        in_specs=[hbm] * 6,
        out_specs=(vmem,) * 4,
        scratch_shapes=[
            V((4, 1536), BF),
            V((4, 1536), BF),
            pltpu.SMEM((1, 1, 18), jnp.int32),
            pltpu.SMEM((1, 1, 18), jnp.int32),
            V((18, 128, 128), BF),
            V((18, 128, 128), BF),
            V((1536, 768), BF),
            V((768, 1536), BF),
            V((8, 8, 48, 128), BF),
            V((8, 8, 48, 128), BF),
            V((3072, 128), F32),
            V((3072, 128), F32),
            V((4, 64, 1536), BF),
            V((4, 64, 1536), BF),
            V((12, 256, 128), BF),
            V((12, 256, 128), BF),
            V((4, 2, 2, 64, 384), F32),
            V((4, 2, 64, 384), F32),
            V((4, 4, 2, 16, 384), BF),
            V((4, 4, 2, 16, 384), BF),
            V((4, 64, 768), BF),
            V((4, 64, 768), BF),
            V((3, 64, 128), F32),
            V((3, 64, 128), F32),
            V((6, 256, 128), BF),
            V((6, 256, 128), BF),
            V((3072, 128), F32),
            V((3072, 128), F32),
            V((3, 4, 384, 128), BF),
            V((3, 4, 384, 128), BF),
            V((3, 4, 384, 128), BF),
            V((3, 4, 384, 128), BF),
            V((384, 128), BF),
            V((8, 48, 128), BF),
            V((384, 128), BF),
            V((8, 48, 128), BF),
            V((48, 128), F32),
            pltpu.SemaphoreType.DMA((N_COPIES,)),
            pltpu.SemaphoreType.DMA((N_COPIES,)),
            pltpu.SemaphoreType.DMA((8,)),
        ],
        compiler_params=pltpu.CompilerParams(
            collective_id=0, has_side_effects=True, vmem_limit_bytes=40 * 1024 * 1024
        ),
    )(
        *(
            pltpu.with_memory_space_constraint(a, pltpu.HBM)
            for a in (tokens, out_grad, up_tiles, down_tiles, up_slots, down_slots)
        )
    )
    return pl.pallas_call(
        write_out,
        out_shape=tuple(jax.ShapeDtypeStruct(r.shape, r.dtype) for r in results),
        in_specs=[vmem] * 4,
        out_specs=(hbm,) * 4,
        scratch_shapes=[pltpu.SemaphoreType.DMA((4,))],
        compiler_params=pltpu.CompilerParams(vmem_limit_bytes=4 * 1024 * 1024),
    )(*(pltpu.with_memory_space_constraint(r, pltpu.VMEM) for r in results))


def solution(mesh):
    spec2, spec5, spec3 = P("hid", "wid"), P("hid", "wid", None, None, None), P("hid", "wid", None)
    return jax.shard_map(
        per_device,
        mesh=mesh,
        in_specs=(spec2, spec2, spec5, spec5, spec3, spec3),
        out_specs=(spec2, spec2, spec5, spec5),
        check_vma=False,
    )
```

```python
import functools

import jax
import jax.numpy as jnp
from jax import lax
from jax.experimental import pallas as pl
from jax.experimental.pallas import tpu as pltpu
from jax.sharding import PartitionSpec as P

MESH = pl.DeviceIdType.MESH
BF = jnp.bfloat16
F32 = jnp.float32

ROOT = 0.7978845608028654
CUBIC = 0.044715

NEAR = (0, 1, 3, 2)
FAR = (2, 3, 1, 0)
ORDER = FAR
SKIP = (1, 2, 3)
REACH = ((4, 3), (3, 3), (3, 3), (3, 3))
SHORT = ()
SUMS = ((4, 3),) * 4


def gelu_both(v):
    inner = jnp.tanh(ROOT * (v + CUBIC * v * v * v))
    value = 0.5 * v * (1.0 + inner)
    slope = 0.5 * (1.0 + inner) + 0.5 * v * (1.0 - inner * inner) * ROOT * (
        1.0 + 3.0 * CUBIC * v * v
    )
    return value, slope


def up8(v):
    return lax.rem(v + 16, 8)


def drain(sent, stores):
    for cp in sent:
        cp.wait_send()
    for cp in stores:
        cp.wait()


def write_out(a, b, c, d, oa, ob, oc, od, sem):
    copies = [
        pltpu.make_async_copy(src, dst, sem.at[n])
        for n, (src, dst) in enumerate(((a, oa), (b, ob), (c, oc), (d, od)))
    ]
    for cp in copies:
        cp.start()
    for cp in copies:
        cp.wait()


def kernel(
    x_hbm, g_hbm, ut_hbm, dt_hbm, us_hbm, ds_hbm,
    mixed_out, gt_out, gu, gd,
    x_in, g_in, us, ds, ut, dt, w1, w2, xcar, gcar, xflat, gflat, xs, gs, xt, gt,
    part, rcore, sb, rx, hb, db, slopes, backs, htile, dtile,
    mcar, tcar, msend, mrecv, tsend, trecv, ms2, mr2, ts2, tr2, rows4,
    ssem, rsem, lsem,
):
    hid, wid = lax.axis_index("hid"), lax.axis_index("wid")
    z, y = lax.div(hid, 8), lax.rem(hid, 8)
    xx, c = lax.div(wid, 2), lax.rem(wid, 2)

    def at(zz, yy):
        return (up8(zz) * 8 + up8(yy), wid)

    def pair(pos, k):
        q = lax.div(pos, 2)
        return (q, q + 1 - 2 * lax.rem(q, 2), lax.rem(q + 2, 4), 3 - q)[k]

    def mate(pos, k, b):
        low = lax.rem(pos, 2)
        return pair(pos, k) * 2 + (1 - low if b else low)

    others = [(k, b) for k in NEAR for b in (0, 1) if (k, b) != (0, 0)]
    xpeer = [(hid, lax.rem(xx + o, 4) * 2 + c) for o in (1, 2, 3)]
    xcross = [(hid, lax.rem(xx + o, 4) * 2 + 1 - c) for o in (1, 2, 3)]
    partner = (hid, xx * 2 + 1 - c)

    counter = [0]
    sent = []
    stores = []

    def rcopy(src, dst, dev):
        k = counter[0]
        counter[0] += 1
        cp = pltpu.make_async_remote_copy(
            src_ref=src, dst_ref=dst, send_sem=ssem.at[k], recv_sem=rsem.at[k],
            device_id=dev, device_id_type=MESH,
        )
        cp.start()
        sent.append(cp)
        return cp

    barrier = pltpu.get_barrier_semaphore()
    peers = [at(z, mate(y, k, b)) for k, b in others] + [at(mate(z, k, b), y) for k, b in others]
    peers += xpeer + xcross + [partner]
    for dev in peers:
        pl.semaphore_signal(barrier, inc=1, device_id=dev, device_id_type=MESH)

    loads = [
        pltpu.make_async_copy(a, b, lsem.at[n])
        for n, (a, b) in enumerate(
            (
                (x_hbm, x_in), (g_hbm, g_in), (us_hbm, us), (ds_hbm, ds),
                (ut_hbm.at[0, 0], ut), (dt_hbm.at[0, 0], dt),
            )
        )
    ]
    for cp in loads:
        cp.start()

    def to_rows(src, dst):
        val = src[...].astype(F32)
        for r in range(12):
            rows4[4 * r : 4 * r + 4, :] = val[:, r * 128 : (r + 1) * 128]
        dst[...] = rows4[...].astype(BF)

    loads[0].wait()
    to_rows(x_in, xcar.at[z, y])
    loads[1].wait()
    to_rows(g_in, gcar.at[y, z])
    pl.semaphore_wait(barrier, len(peers))

    first = {}
    for k, b in others:
        first["x", k, b] = rcopy(xcar.at[z, y], xcar.at[z, y], at(z, mate(y, k, b)))
        first["g", k, b] = rcopy(gcar.at[y, z], gcar.at[y, z], at(mate(z, k, b), y))

    for cp in loads[2:]:
        cp.wait()

    def build(slots, tiles, dense, rows, cols):
        def one(row, carry):
            pos = jnp.int32(0)
            for n in range(18):
                pos = pos + (slots[0, 0, n] < row * cols).astype(jnp.int32)
            for col in range(cols):
                idx = jnp.minimum(pos, 17)
                hit = jnp.logical_and(pos < 18, slots[0, 0, idx] == row * cols + col)
                tile = tiles[idx]
                dense[
                    pl.ds(pl.multiple_of(row * 128, 128), 128), col * 128 : (col + 1) * 128
                ] = jnp.where(hit, tile, jnp.zeros_like(tile))
                pos = pos + hit.astype(jnp.int32)
            return carry

        lax.fori_loop(0, rows, one, jnp.int32(0))

    build(us, ut, w1, 12, 6)
    build(ds, dt, w2, 6, 12)

    axes = {
        "x": (xcar, z, y, lambda d: at(z + d, y)),
        "g": (gcar, y, z, lambda d: at(z, y + d)),
    }
    ring = {}

    def offsets(g):
        return (-g, g + 1)

    def settle(keep=0):
        for cp in sent[: len(sent) - keep]:
            cp.wait_send()
        del sent[: len(sent) - keep]

    def run(tasks, share):
        for _ in range(min(len(tasks), share)):
            tasks.pop(0)()

    def step(s, tasks=()):
        tasks = list(tasks)
        share = -(-len(tasks) // 5)
        run(tasks, share)
        for k in NEAR:
            for name in ("x", "g"):
                car, pos, cross, dev = axes[name]
                span = pl.ds(pair(cross, k) * 2, 2)

                def forward(slab, hops, key):
                    ref = car.at[up8(slab), span]
                    ring[(name, k) + key] = rcopy(ref, ref, dev(hops))

                if s == 0:
                    for b in (0, 1):
                        if (k, b) != (0, 0):
                            first[name, k, b].wait_recv()
                else:
                    for way in (0, 1):
                        if s <= REACH[k][way]:
                            ring[name, k, s - 1, way].wait_recv()
                    if s == 4 and k in SKIP:
                        ring[name, k, 2, 2].wait_recv()
                if s == 2 and k in SKIP:
                    way = -1 if k == 3 else 1
                    forward(pos - 2 * way, 2 * way, (2, 2))
                for way in (0, 1):
                    if s < REACH[k][way]:
                        sign = 1 - 2 * way
                        forward(pos - sign * s, sign, (s, way))
            run(tasks, share)

    def widen(car, pos, flat, off):
        d = up8(pos + off)
        flat[pl.ds(pl.multiple_of(d * 384, 384), 384), :] = car[d].reshape(384, 128).astype(F32)

    def unpack(pos, flat, dst, g, tiles):
        for r in tiles:
            for i in range(4):
                rows = [
                    flat[pl.ds(up8(pos + off) * 384 + 4 * r + i, 8, stride=48), :]
                    for off in offsets(g)
                ]
                dst[g, i * 16 : (i + 1) * 16, r * 128 : (r + 1) * 128] = jnp.concatenate(
                    rows, axis=0
                ).astype(BF)

    core = {}
    over = {}
    back_home = {}

    def product(a, g, q):
        cols = slice(q * 256, (q + 1) * 256)
        if a == 0:
            val = jnp.dot(xs[g], w1[:, cols], preferred_element_type=F32)
        else:
            val = lax.dot_general(
                gs[g], w2[cols, :], (((1,), (1,)), ((), ())), preferred_element_type=F32
            )
        for t in range(2):
            n = 2 * q + t
            part[g, n // 3, a, :, (n % 3) * 128 : (n % 3 + 1) * 128] = val[
                :, t * 128 : (t + 1) * 128
            ]
        if q == 2:
            core[g, a] = rcopy(part.at[g, 1 - c, a], rcore.at[g, a], partner)

    def compute(g, a):
        car, pos, flat, dst = ((xcar, z, xflat, xs), (gcar, y, gflat, gs))[a]
        tasks = [functools.partial(widen, car, pos, flat, off) for off in offsets(g)]
        for t in range(4):
            tasks.append(
                functools.partial(unpack, pos, flat, dst, g, (3 * t, 3 * t + 1, 3 * t + 2))
            )
        return tasks + [functools.partial(product, a, g, q) for q in range(3)]

    def compute_now(g, a):
        for task in compute(g, a):
            task()

    def sum_cores(g, a):
        core[g, a].wait_recv()
        total = part[g, c, a] + rcore[g, a]
        rcore[g, a] = total
        for i in range(4):
            sb[g, i, a] = total[i * 16 : (i + 1) * 16].astype(BF)
        for dev, o in zip(xpeer, (1, 2, 3)):
            over[g, a, o] = rcopy(sb.at[g, lax.rem(xx + o, 4), a], rx.at[g, o, a], dev)

    def mine(buf, g, i):
        return buf.at[
            g,
            pl.ds(pl.multiple_of(i * 16, 16), 16),
            pl.ds(pl.multiple_of(c * 384, 128), 384),
        ]

    def send_home(buf, name, g):
        ref = mine(buf, g, xx)
        devs = xpeer + [partner] + (xcross if g == 3 else [])
        back_home[name, g] = [rcopy(ref, ref, dev) for dev in devs]

    def relay(buf, name, g):
        for n, o in enumerate((1, 2, 3)):
            back_home[name, g][n].wait_recv()
            ref = mine(buf, g, lax.rem(xx + 4 - o, 4))
            back_home[name, g].append(rcopy(ref, ref, partner))

    def all_home(name, g):
        for cp in back_home[name, g][0 if g == 3 else 3 :]:
            cp.wait_recv()

    def sum_chips(g, a):
        acc = rcore[g, a, pl.ds(pl.multiple_of(xx * 16, 16), 16), :]
        for o in (1, 2, 3):
            over[g, a, o].wait_recv()
            acc = acc + rx[g, o, a].astype(F32)
        return acc

    def lay(buf, val, pos, g):
        for n, off in enumerate(offsets(g)):
            d = up8(pos + off)
            for t in range(3):
                buf[t, pl.ds(pl.multiple_of(d * 8, 8), 8), :] = val[
                    n * 8 : (n + 1) * 8, t * 128 : (t + 1) * 128
                ]

    def hidden(g):
        value, slope = gelu_both(sum_chips(g, 0))
        ref = mine(hb, g, xx)
        ref[...] = value.astype(BF)
        send_home(hb, "h", g)
        lay(slopes, slope, z, g)

    def delta(g):
        lay(backs, sum_chips(g, 1), y, g)
        rows = []
        for off in offsets(g):
            dy = up8(y + off)
            rows.append(
                jnp.concatenate(
                    [
                        backs[t, pl.ds(pl.multiple_of(dy * 8, 8), 8), :]
                        * slopes[t, pl.ds(dy, 8, stride=8), :]
                        for t in range(3)
                    ],
                    axis=1,
                )
            )
        ref = mine(db, g, xx)
        ref[...] = jnp.concatenate(rows, axis=0).astype(BF)
        send_home(db, "d", g)

    def retile(flat, pos, dst):
        def one(g, carry):
            for r in range(12):
                for i in range(4):
                    rows = [
                        flat[pl.ds(up8(pos - g + n * (2 * g + 1)) * 48 + 4 * r + i, 8, stride=384), :]
                        for n in range(2)
                    ]
                    dst[r, pl.ds(pl.multiple_of(g * 64 + i * 16, 16), 16), :] = jnp.concatenate(
                        rows, axis=0
                    ).astype(BF)
            return carry

        lax.fori_loop(0, 4, one, jnp.int32(0))

    def pack(val, r, car, pos, groups):
        for n, g in enumerate(groups):
            for i in range(4):
                for m, off in enumerate(offsets(g)):
                    lo = n * 64 + i * 16 + m * 8
                    car[pl.ds(up8(pos + off) * 384 + 4 * r + i, 8, stride=48), :] = val[lo : lo + 8]

    def mixed_part(groups):
        lhs = jnp.concatenate([hb[g] for g in groups], axis=0)

        def cols(q, carry):
            val = jnp.dot(
                lhs, w2[:, pl.ds(pl.multiple_of(q * 256, 256), 256)], preferred_element_type=F32
            )
            pack(val[:, :128], 2 * q, mcar, z, groups)
            pack(val[:, 128:], 2 * q + 1, mcar, z, groups)
            return carry

        for q in range(6):
            cols(q, 0)

    def back_part(groups):
        lhs = jnp.concatenate([db[g] for g in groups], axis=0)

        def cols(q, carry):
            val = lax.dot_general(
                lhs,
                w1[pl.ds(pl.multiple_of(q * 256, 256), 256), :],
                (((1,), (1,)), ((), ())),
                preferred_element_type=F32,
            )
            pack(val[:, :128], 2 * q, tcar, y, groups)
            pack(val[:, 128:], 2 * q + 1, tcar, y, groups)
            return carry

        for q in range(6):
            cols(q, 0)

    outs = {
        "m": (mcar, msend, mrecv, z, y, lambda d: at(z + d, y), ms2, mr2),
        "t": (tcar, tsend, trecv, y, z, lambda d: at(z, y + d), ts2, tr2),
    }
    rsum = {}
    last = {}

    def block(name, k, d):
        car, pos, cross = outs[name][0], outs[name][3], outs[name][4]
        return pl.ds(pl.multiple_of(up8(pos + d) * 384 + pair(cross, k) * 96, 96), 96)

    def span_of(name, k):
        return pl.ds(pl.multiple_of(pair(outs[name][4], k) * 96, 96), 96)

    def got(name, k, way, s):
        rsum[name, k, way, s].wait_recv()
        return outs[name][2][way, s, span_of(name, k), :].astype(F32)

    def ring_send(name, k, s):
        car, send, recv, pos, cross, dev, _, _ = outs[name]
        span = span_of(name, k)

        def push(val, way, hops):
            send[way, s, span, :] = val.astype(BF)
            rsum[name, k, way, s] = rcopy(
                send.at[way, s, span, :], recv.at[way, s, span, :], dev(hops)
            )

        far_way = SHORT.index(k) if k in SHORT else None
        if s == 0 and k in SHORT:
            push(car[block(name, k, 4), :], 2, 2 - 4 * far_way)
        for way in (0, 1):
            reach = SUMS[k][way] - s
            if reach < 1:
                continue
            val = car[block(name, k, reach if way == 0 else -reach), :]
            if s > 0:
                val = val + got(name, k, way, s - 1)
            if s == 1 and far_way == way:
                val = val + got(name, k, 2, 0)
            push(val, way, 1 - 2 * way)

    def ring_end(name, k):
        car, _, _, pos, cross, _, send2, recv2 = outs[name]
        span = span_of(name, k)
        here = block(name, k, 0)
        val = car[here, :] + got(name, k, 0, SUMS[k][0] - 1) + got(name, k, 1, SUMS[k][1] - 1)
        car[here, :] = val
        send2[span, :] = val.astype(BF)
        for b in (0, 1):
            if (k, b) == (0, 0):
                continue
            to = mate(cross, k, b)
            dev = at(pos, to) if name == "m" else at(to, pos)
            last[name, k, b] = rcopy(
                send2.at[pl.ds(pl.multiple_of(to * 48, 48), 48), :], recv2.at[2 * k + b], dev
            )

    def ring_step(s, names=("m", "t"), pairs=ORDER):
        turns = sorted(
            (n + 2 * names.index(name), names.index(name), name, k)
            for n, k in enumerate(pairs)
            for name in names
        )
        for _, _, name, k in turns:
            if s == 4:
                ring_end(name, k)
            else:
                ring_send(name, k, s)

    def up_some(lo, hi):
        def one(n):
            slot = us[0, 0, n]
            lhs, rhs = xt[lax.div(slot, 6)], dtile[lax.rem(slot, 6)]
            gu[0, 0, n] = lax.dot_general(
                lhs, rhs, (((0,), (0,)), ((), ())), preferred_element_type=F32
            )

        def six(t, carry):
            for n in range(6):
                one(lo + 6 * t + n)
            return carry

        lax.fori_loop(0, (hi - lo) // 6, six, jnp.int32(0))

    def down_some(lo, hi):
        def one(n):
            slot = ds[0, 0, n]
            lhs, rhs = htile[lax.div(slot, 12)], gt[lax.rem(slot, 12)]
            gd[0, 0, n] = lax.dot_general(
                lhs, rhs, (((0,), (0,)), ((), ())), preferred_element_type=F32
            )

        def six(t, carry):
            for n in range(6):
                one(lo + 6 * t + n)
            return carry

        lax.fori_loop(0, (hi - lo) // 6, six, jnp.int32(0))

    def tile_up(buf, dst):
        for b in range(6):
            dst[b] = buf[:, :, b * 128 : (b + 1) * 128].reshape(256, 128)

    P_ = functools.partial
    step(0)
    step(1)
    step(2, compute(0, 0))
    todo = compute(1, 0)
    step(3, todo[:5] + [P_(sum_cores, 0, 0)] + todo[5:])
    todo = compute(2, 0)
    step(4, todo[:5] + [P_(sum_cores, 1, 0)] + todo[5:])
    compute_now(3, 0)
    sum_cores(2, 0)
    compute_now(3, 1)
    sum_cores(3, 0)
    compute_now(2, 1)
    sum_cores(3, 1)
    hidden(0)
    compute_now(1, 1)
    sum_cores(2, 1)
    hidden(1)
    compute_now(0, 1)
    sum_cores(1, 1)
    hidden(2)
    sum_cores(0, 1)
    relay(hb, "h", 0)
    hidden(3)
    delta(3)
    relay(hb, "h", 1)
    delta(2)
    delta(1)
    delta(0)
    for g in (1, 0):
        all_home("h", g)
    mixed_part((1, 0))
    settle(60)
    relay(hb, "h", 2)
    all_home("h", 3)
    mixed_part((3,))
    ring_step(0, names=("m",))
    all_home("d", 3)
    back_part((3,))
    ring_step(0, names=("t",))
    relay(db, "d", 2)
    all_home("h", 2)
    mixed_part((2,))
    all_home("d", 2)
    back_part((2,))
    ring_step(1)
    relay(db, "d", 1)
    relay(db, "d", 0)
    for g in (1, 0):
        all_home("d", g)
    back_part((1, 0))
    ring_step(2)
    settle(40)
    retile(xflat, y, xt)
    ring_step(3)
    tile_up(db, dtile)
    up_some(0, 12)
    ring_step(4)
    tile_up(hb, htile)
    retile(gflat, z, gt)
    up_some(12, 18)
    down_some(0, 18)
    settle(14)

    def finish(name, recv2, out):
        car, _, _, pos, cross, _, _, _ = outs[name]
        acc = car[pl.ds(pl.multiple_of(pos * 384 + cross * 48, 48), 48), :]
        for k, b in others:
            last[name, k, b].wait_recv()
            acc = acc + recv2[2 * k + b].astype(F32)
        rows4[...] = acc
        cols = [rows4[4 * r : 4 * r + 4, :] for r in range(12)]
        out[...] = jnp.concatenate(cols, axis=1).astype(BF)

    finish("m", mr2, mixed_out)
    finish("t", tr2, gt_out)
    drain(sent, stores)


N_COPIES = 14 + 56 + 8 + 24 + 56 + 56 + 14 + 16


def per_device(tokens, out_grad, up_tiles, down_tiles, up_slots, down_slots):
    vmem = pl.BlockSpec(memory_space=pltpu.VMEM)
    hbm = pl.BlockSpec(memory_space=pltpu.HBM)
    V = pltpu.VMEM
    results = pl.pallas_call(
        kernel,
        out_shape=(
            V((4, 1536), BF),
            V((4, 1536), BF),
            V((1, 1, 18, 128, 128), F32),
            V((1, 1, 18, 128, 128), F32),
        ),
        in_specs=[hbm] * 6,
        out_specs=(vmem,) * 4,
        scratch_shapes=[
            V((4, 1536), BF),
            V((4, 1536), BF),
            pltpu.SMEM((1, 1, 18), jnp.int32),
            pltpu.SMEM((1, 1, 18), jnp.int32),
            V((18, 128, 128), BF),
            V((18, 128, 128), BF),
            V((1536, 768), BF),
            V((768, 1536), BF),
            V((8, 8, 48, 128), BF),
            V((8, 8, 48, 128), BF),
            V((3072, 128), F32),
            V((3072, 128), F32),
            V((4, 64, 1536), BF),
            V((4, 64, 1536), BF),
            V((12, 256, 128), BF),
            V((12, 256, 128), BF),
            V((4, 2, 2, 64, 384), F32),
            V((4, 2, 64, 384), F32),
            V((4, 4, 2, 16, 384), BF),
            V((4, 4, 2, 16, 384), BF),
            V((4, 64, 768), BF),
            V((4, 64, 768), BF),
            V((3, 64, 128), F32),
            V((3, 64, 128), F32),
            V((6, 256, 128), BF),
            V((6, 256, 128), BF),
            V((3072, 128), F32),
            V((3072, 128), F32),
            V((3, 4, 384, 128), BF),
            V((3, 4, 384, 128), BF),
            V((3, 4, 384, 128), BF),
            V((3, 4, 384, 128), BF),
            V((384, 128), BF),
            V((8, 48, 128), BF),
            V((384, 128), BF),
            V((8, 48, 128), BF),
            V((48, 128), F32),
            pltpu.SemaphoreType.DMA((N_COPIES,)),
            pltpu.SemaphoreType.DMA((N_COPIES,)),
            pltpu.SemaphoreType.DMA((8,)),
        ],
        compiler_params=pltpu.CompilerParams(
            collective_id=0, has_side_effects=True, vmem_limit_bytes=40 * 1024 * 1024
        ),
    )(
        *(
            pltpu.with_memory_space_constraint(a, pltpu.HBM)
            for a in (tokens, out_grad, up_tiles, down_tiles, up_slots, down_slots)
        )
    )
    return pl.pallas_call(
        write_out,
        out_shape=tuple(jax.ShapeDtypeStruct(r.shape, r.dtype) for r in results),
        in_specs=[vmem] * 4,
        out_specs=(hbm,) * 4,
        scratch_shapes=[pltpu.SemaphoreType.DMA((4,))],
        compiler_params=pltpu.CompilerParams(vmem_limit_bytes=4 * 1024 * 1024),
    )(*(pltpu.with_memory_space_constraint(r, pltpu.VMEM) for r in results))


def solution(mesh):
    spec2, spec5, spec3 = P("hid", "wid"), P("hid", "wid", None, None, None), P("hid", "wid", None)
    return jax.shard_map(
        per_device,
        mesh=mesh,
        in_specs=(spec2, spec2, spec5, spec5, spec3, spec3),
        out_specs=(spec2, spec2, spec5, spec5),
        check_vma=False,
    )
```
